512 devices in a mesh: seq: 64 (over x_hi, z, core), tp: 8 (over x_lo, y).
Axes of the slice: x: 4 (x_hi: 2, x_lo: 2; x = x_hi * 2 + x_lo), y: 4, z: 16, core: 2. Of those that a mesh axis runs over, the one named last changes fastest.
Arguments:
- queries: bfloat16 [8192, 8192], P('seq', 'tp'), may hold values from -6 to 6
- keys: bfloat16 [8192, 8192], P('seq', 'tp'), may hold values from -6 to 6
- values: bfloat16 [8192, 8192], P('seq', 'tp'), may hold values from -6 to 6
- short_taps: float32 [3, 3, 8192], P(None, None, 'tp'), may hold values from -3 to 3
- long_filter: float32 [8192, 8192], P(('tp', 'seq')), may hold values from -8 to 8
- out_weight: bfloat16 [8192, 4096], P('seq', 'tp'), may hold values from -0.0625 to 0.0625
- cotangent: bfloat16 [8192, 4096], P('seq', 'tp'), may hold values from -6 to 6
Outputs:
- mixed: bfloat16 [8192, 4096], P('seq', 'tp')
- query_grad: bfloat16 [8192, 8192], P('seq', 'tp')
- key_grad: bfloat16 [8192, 8192], P('seq', 'tp')
- value_grad: bfloat16 [8192, 8192], P('seq', 'tp')
- filter_grad: float32 [8192, 8192], P(('tp', 'seq'))
The draws below stay inside these ranges and needn't reach their ends.
All inputs are finite; a program needn't handle non-finite values.
Results may differ from the reference program's by a relative error of at most 0.023.
Values may be sent and summed in bfloat16 or wider, within the bound.
No kernel may reach another device: no remote copies, remote signals or barrier semaphores. Data moves between devices by JAX's collectives and lax.ppermute only.
A program may use at most 64 MiB of HBM per device.

```python
import math
import jax
import jax.numpy as jnp
from jax import lax

C = 8192
D = 4096
TAPS = 3
TOKEN_COUNT = 8192
N_TP = 8


def draw_long_filter(key, part):
    key = jax.random.fold_in(key, 11)
    damping_speed_seed, payload_draw_seed, spike_draw_seed, magnitude_draw_seed = jax.random.split(key, 4)
    lowest, highest = (0.004, 50.0)
    entries = jax.random.truncated_normal(payload_draw_seed, -4.0, 4.0, (C, TOKEN_COUNT), jnp.float32)
    ratio = jnp.exp(jax.random.uniform(damping_speed_seed, (C, 1), jnp.float32, math.log(lowest), math.log(highest)))
    reach = ratio * TOKEN_COUNT
    positions = jnp.arange(TOKEN_COUNT, dtype=jnp.int32)
    times = positions.astype(jnp.float32)[None, :]
    kernel_anchor_points = jax.random.randint(spike_draw_seed, (3,), 1, TOKEN_COUNT)
    drops = jnp.ones((TOKEN_COUNT,), jnp.float32)
    for spot_index in range(3):
        drops = drops * jnp.where(positions >= kernel_anchor_points[spot_index], 0.6, 1.0)
    scaling = jnp.sqrt((1.0 - jnp.exp(-2.0 / reach)) / (1.0 - jnp.exp(-2.0 * TOKEN_COUNT / reach)))
    amplitude = jnp.exp(jax.random.uniform(magnitude_draw_seed, (C, 1), jnp.float32, math.log(0.5), math.log(2.0)))
    return entries * jnp.exp(-times / reach) * scaling * amplitude * drops[None, :]


def steps_of(own_key, shape, cuts, least, top_value):
    loudness = 1.0
    for position, shards_of in cuts:
        draws = jax.random.uniform(jax.random.fold_in(jax.random.fold_in(own_key, 6), position), (shards_of,), jnp.float32, least / len(cuts), top_value / len(cuts))
        loudness = loudness * jnp.repeat(jnp.exp(draws), shape[position] // shards_of).reshape((-1,) + (1,) * (len(shape) - 1 - position))
    return loudness


def bell_draw(own_key, dims, deviation, most, cuts=(), kind=jnp.bfloat16):
    values = jax.random.normal(own_key, dims, jnp.float32) * deviation
    if len(cuts) > 0:
        values = steps_of(own_key, dims, cuts, -0.22, 0.18) * values
    return jnp.clip(values, min=-most, max=most).astype(kind)


def setup_inputs(seed: int = 0) -> dict:
    splits = jax.random.split(jax.random.key(seed), 8)
    queries = bell_draw(splits[0], (TOKEN_COUNT, C), 1.0, 6.0, ((0, 64), (1, 8)))
    keys = bell_draw(splits[1], (TOKEN_COUNT, C), 1.0, 6.0, ((0, 64), (1, 8)))
    values = bell_draw(splits[2], (TOKEN_COUNT, C), 1.0, 6.0, ((0, 64), (1, 8)))
    short_taps = bell_draw(splits[3], (3, TAPS, C), 0.6, 3.0, ((2, 8),), jnp.float32)
    long_filter = draw_long_filter(jax.random.fold_in(splits[7], 71), 0)
    out_weight = bell_draw(splits[5], (C, D), C ** -0.5, 0.0625, ((0, 64), (1, 8)))
    cotangent = bell_draw(splits[6], (TOKEN_COUNT, D), 1.0, 6.0, ((0, 64), (1, 8)))
    return {"queries": queries, "keys": keys, "values": values, "short_taps": short_taps, "long_filter": long_filter, "out_weight": out_weight, "cotangent": cotangent}


def causal_taps(signal, taps):
    rim_rows = taps.shape[0] - 1
    padded = jnp.pad(signal, ((rim_rows, 0), (0, 0)))
    result = jnp.zeros_like(signal)
    for tap_index in range(taps.shape[0]):
        first_row = rim_rows - tap_index
        result = result + taps[tap_index][None, :] * padded[first_row:first_row + signal.shape[0]]
    return result

def adjoint_taps(signal, taps):
    rim_rows = taps.shape[0] - 1
    padded = jnp.pad(signal, ((0, rim_rows), (0, 0)))
    result = jnp.zeros_like(signal)
    for tap_index in range(taps.shape[0]):
        result = result + taps[tap_index][None, :] * padded[tap_index:tap_index + signal.shape[0]]
    return result

def reference(queries, keys, values, short_taps, long_filter, out_weight, cotangent):
    query_conv = causal_taps(queries.astype(jnp.float32), short_taps[0])
    key_conv = causal_taps(keys.astype(jnp.float32), short_taps[1])
    value_conv = causal_taps(values.astype(jnp.float32), short_taps[2])
    product = (key_conv * value_conv).astype(jnp.bfloat16)
    block_rows = min(C, 512)
    groups = C // block_rows
    padded_length = 2 * TOKEN_COUNT
    filter_blocks = long_filter.reshape(groups, block_rows, TOKEN_COUNT)
    product_blocks = product.astype(jnp.float32).T.reshape(groups, block_rows, TOKEN_COUNT)

    def forward_block(operands):
        filter_rows, signal_rows = operands
        spectrum = jnp.fft.rfft(filter_rows, padded_length) * jnp.fft.rfft(signal_rows, padded_length)
        return jnp.fft.irfft(spectrum, padded_length)[:, :TOKEN_COUNT]
    convolved = lax.map(forward_block, (filter_blocks, product_blocks)).reshape(C, TOKEN_COUNT)
    long_out = convolved.T.astype(jnp.bfloat16)
    long_float = long_out.astype(jnp.float32)
    gated = (query_conv * long_float).astype(jnp.bfloat16)
    mixed = jnp.dot(gated, out_weight, preferred_element_type=jnp.float32).astype(jnp.bfloat16)
    group_width = D // N_TP
    gated_grad = jnp.zeros((TOKEN_COUNT, C), jnp.float32)
    for group_index in range(N_TP):
        low = group_index * group_width
        piece = jnp.dot(cotangent[:, low:low + group_width], out_weight[:, low:low + group_width].T, preferred_element_type=jnp.float32)
        gated_grad = gated_grad + piece.astype(jnp.bfloat16).astype(jnp.float32)
    long_grad = (query_conv * gated_grad).astype(jnp.bfloat16)
    question_smoothing_derivative = gated_grad * long_float
    grad_blocks = long_grad.astype(jnp.float32).T.reshape(groups, block_rows, TOKEN_COUNT)

    def backward_block(operands):
        filter_rows, signal_rows, grad_rows = operands
        grad_spectrum = jnp.fft.rfft(grad_rows, padded_length)
        filter_spectrum = jnp.fft.rfft(filter_rows, padded_length)
        signal_spectrum = jnp.fft.rfft(signal_rows, padded_length)
        to_product = jnp.fft.irfft(jnp.conj(filter_spectrum) * grad_spectrum, padded_length)[:, :TOKEN_COUNT]
        to_filter = jnp.fft.irfft(jnp.conj(signal_spectrum) * grad_spectrum, padded_length)[:, :TOKEN_COUNT]
        return (to_product, to_filter)
    product_back, filter_back = lax.map(backward_block, (filter_blocks, product_blocks, grad_blocks))
    product_grad = product_back.reshape(C, TOKEN_COUNT).T.astype(jnp.bfloat16)
    filter_grad = filter_back.reshape(C, TOKEN_COUNT) / math.sqrt(TOKEN_COUNT)
    product_float = product_grad.astype(jnp.float32)
    key_conv_grad = product_float * value_conv
    value_conv_grad = product_float * key_conv
    query_grad = adjoint_taps(question_smoothing_derivative, short_taps[0]).astype(jnp.bfloat16)
    key_grad = adjoint_taps(key_conv_grad, short_taps[1]).astype(jnp.bfloat16)
    value_grad = adjoint_taps(value_conv_grad, short_taps[2]).astype(jnp.bfloat16)
    return (mixed, query_grad, key_grad, value_grad, filter_grad)
```

```python
import functools
import math

import jax
import jax.numpy as jnp
import numpy as np
from jax import lax
from jax.experimental import pallas as pl
from jax.experimental.pallas import tpu as pltpu
from jax.sharding import Mesh
from jax.sharding import PartitionSpec as P

BF16 = jnp.bfloat16
F32 = jnp.float32

SEQ = ("xh", "z", "co")
TP = ("xl", "y")
PLANE = ("xh", "y")
COLUMN = ("z", "co")

CHANNELS = 16
BLOCKS = 64
LANES = 128
LENGTH = BLOCKS * LANES


def transform_tables():
    blocks = np.arange(BLOCKS)
    lanes = np.arange(LANES)
    first = 2.0 * np.pi * np.outer(blocks + 0.25, blocks) / BLOCKS
    twist = 2.0 * np.pi * np.outer(blocks + 0.25, lanes) / LENGTH
    second = 2.0 * np.pi * (np.outer(lanes, lanes) % LANES) / LANES
    first_table = np.concatenate([np.cos(first), -np.sin(first)], axis=0)
    cosine, sine = np.cos(second), np.sin(second)
    second_table = np.block([[cosine, -sine], [sine, cosine]])
    return (
        jnp.asarray(first_table, BF16),
        jnp.asarray(first_table.T / LENGTH, BF16),
        jnp.asarray(np.cos(twist), F32),
        jnp.asarray(np.sin(twist), F32),
        jnp.asarray(second_table, BF16),
        jnp.asarray(second_table.T, BF16),
    )


def to_spectrum(grid_ref, turned_ref, first, cos_twist, sin_twist, second):
    for c in range(CHANNELS):
        grid = grid_ref[pl.ds(c, BLOCKS, stride=CHANNELS), :].astype(BF16)
        section = jnp.dot(first, grid, preferred_element_type=F32)
        real, imag = section[:BLOCKS], section[BLOCKS:]
        rows = slice(c * BLOCKS, (c + 1) * BLOCKS)
        turned_ref[rows, :LANES] = (real * cos_twist + imag * sin_twist).astype(BF16)
        turned_ref[rows, LANES:] = (imag * cos_twist - real * sin_twist).astype(BF16)
    return jnp.dot(turned_ref[...], second, preferred_element_type=F32)


def from_spectrum(spectrum, grid_ref, section_ref, first_back, cos_twist, sin_twist, second_back):
    section_ref[...] = jnp.dot(spectrum, second_back, preferred_element_type=F32)
    for c in range(CHANNELS):
        rows = slice(c * BLOCKS, (c + 1) * BLOCKS)
        real, imag = section_ref[rows, :LANES], section_ref[rows, LANES:]
        turned = jnp.concatenate(
            [real * cos_twist - imag * sin_twist, imag * cos_twist + real * sin_twist], axis=0
        ).astype(BF16)
        grid_ref[pl.ds(c, BLOCKS, stride=CHANNELS), :] = jnp.dot(
            first_back, turned, preferred_element_type=F32
        )


def filter_kernel(filter_ref, first, cos_twist, sin_twist, second, spectrum_ref, grid, turned):
    for b in range(BLOCKS):
        grid[b * CHANNELS : (b + 1) * CHANNELS, :] = filter_ref[:, b * LANES : (b + 1) * LANES]
    spectrum_ref[...] = to_spectrum(
        grid, turned, first[...], cos_twist[...], sin_twist[...], second[...]
    )


def forward_kernel(
    product_ref, filter_spectrum, first, first_back, cos_twist, sin_twist, second, second_back,
    long_ref, product_spectrum, grid, turned, section,
):
    grid[...] = product_ref[...].astype(F32).reshape(BLOCKS * CHANNELS, LANES)
    own = to_spectrum(grid, turned, first[...], cos_twist[...], sin_twist[...], second[...])
    product_spectrum[...] = own
    own_re, own_im = own[:, :LANES], own[:, LANES:]
    other_re, other_im = filter_spectrum[:, :LANES], filter_spectrum[:, LANES:]
    turned[:, :LANES] = (own_re * other_re - own_im * other_im).astype(BF16)
    turned[:, LANES:] = (own_re * other_im + own_im * other_re).astype(BF16)
    from_spectrum(
        turned[...], grid, section, first_back[...], cos_twist[...], sin_twist[...], second_back[...]
    )
    long_ref[...] = grid[...].reshape(BLOCKS, CHANNELS, LANES).astype(BF16)


def backward_kernel(
    grad_ref, filter_spectrum, product_spectrum,
    first, first_back, cos_twist, sin_twist, second, second_back,
    back_ref, filter_grad_ref, grid, turned, section,
):
    grid[...] = grad_ref[...].astype(F32).reshape(BLOCKS * CHANNELS, LANES)
    own = to_spectrum(grid, turned, first[...], cos_twist[...], sin_twist[...], second[...])
    own_re, own_im = own[:, :LANES], own[:, LANES:]

    def correlate(other):
        other_re, other_im = other[:, :LANES], other[:, LANES:]
        turned[:, :LANES] = (own_re * other_re + own_im * other_im).astype(BF16)
        turned[:, LANES:] = (own_im * other_re - own_re * other_im).astype(BF16)
        from_spectrum(
            turned[...], grid, section, first_back[...], cos_twist[...], sin_twist[...], second_back[...]
        )

    correlate(filter_spectrum)
    back_ref[...] = grid[...].reshape(BLOCKS, CHANNELS, LANES).astype(BF16)
    correlate(product_spectrum)
    for b in range(BLOCKS):
        filter_grad_ref[:, b * LANES : (b + 1) * LANES] = grid[
            b * CHANNELS : (b + 1) * CHANNELS, :
        ] * (1.0 / math.sqrt(LENGTH))


SPECTRUM = jax.ShapeDtypeStruct((CHANNELS * BLOCKS, 2 * LANES), F32)
SEQUENCES = jax.ShapeDtypeStruct((BLOCKS, CHANNELS, LANES), BF16)
GRID = pltpu.VMEM((BLOCKS * CHANNELS, LANES), F32)
TURNED = pltpu.VMEM((CHANNELS * BLOCKS, 2 * LANES), BF16)
SECTION = pltpu.VMEM((CHANNELS * BLOCKS, 2 * LANES), F32)


def run_kernel(kernel, out_shape, scratch, transforms, *operands):
    transform_flops = 2 * CHANNELS * BLOCKS * LANES * (2 * BLOCKS + 4 * LANES)
    return pl.pallas_call(
        kernel,
        out_shape=out_shape,
        scratch_shapes=scratch,
        compiler_params=pltpu.CompilerParams(vmem_limit_bytes=40 * 2**20),
        cost_estimate=pl.CostEstimate(
            flops=transforms * transform_flops, bytes_accessed=4 * 2**20, transcendentals=0
        ),
    )(*operands)


def shift(value, steps):
    count = 1
    for axis in SEQ:
        count *= lax.axis_size(axis)
    first, last = max(0, -steps), min(count, count - steps)
    return lax.ppermute(value, SEQ, [(i, i + steps) for i in range(first, last)])


def across(value, target):
    pairs = [(2 * a + b, 2 * target(a, b)[0] + target(a, b)[1]) for a in range(2) for b in range(2)]
    return lax.ppermute(value, ("xh", "xl"), pairs)


def per_device(queries, keys, values, short_taps, long_filter, out_weight, cotangent):
    rows, width = queries.shape
    taps = short_taps.shape[1]
    rim = taps - 1
    features = out_weight.shape[1]
    half = lax.axis_index("xl")

    weight = lax.all_gather(
        across(out_weight, lambda a, b: (b, a)), COLUMN, axis=0, tiled=True
    ).reshape(4, width, features)
    near = across(cotangent, lambda a, b: (b, a))
    far = across(cotangent, lambda a, b: (b, 1 - a))
    gradient = jnp.where(half == 0, jnp.stack([near, far]), jnp.stack([far, near]))

    first, first_back, cos_twist, sin_twist, second, second_back = transform_tables()
    filter_spectrum = run_kernel(
        filter_kernel, SPECTRUM, [GRID, TURNED], 1, long_filter, first, cos_twist, sin_twist, second
    )

    stacked = jnp.stack([queries, keys, values])
    before = shift(stacked[:, rows - rim :], 1)
    extended = jnp.concatenate([before, stacked], axis=1).astype(F32)
    filtered = jnp.zeros(stacked.shape, F32)
    for tap in range(taps):
        start = rim - tap
        filtered = filtered + short_taps[:, tap][:, None, :] * extended[:, start : start + rows]
    query_conv, key_conv, value_conv = filtered[0], filtered[1], filtered[2]
    product = (key_conv * value_conv).astype(BF16)

    product_owned = lax.all_to_all(product.T.reshape(BLOCKS, CHANNELS, LANES), SEQ, 0, 0, tiled=True)
    long_owned, product_spectrum = run_kernel(
        forward_kernel, [SEQUENCES, SPECTRUM], [GRID, TURNED, SECTION], 2,
        product_owned, filter_spectrum, first, first_back, cos_twist, sin_twist, second, second_back,
    )
    long_out = lax.all_to_all(long_owned, SEQ, 0, 0, tiled=True).reshape(width, rows).T
    long_float = long_out.astype(F32)
    gated = (query_conv * long_float).astype(BF16)

    partial = jnp.einsum(
        "tmk,ynk->tymn", gradient, weight, preferred_element_type=F32
    ).astype(BF16)
    partial = partial.reshape(8, rows, width)
    gated_grad = jnp.sum(lax.all_to_all(partial, PLANE, 0, 0, tiled=True).astype(F32), axis=0)

    long_grad = (query_conv * gated_grad).astype(BF16)
    query_conv_grad = gated_grad * long_float
    grad_owned = lax.all_to_all(long_grad.T.reshape(BLOCKS, CHANNELS, LANES), SEQ, 0, 0, tiled=True)
    back_owned, filter_grad = run_kernel(
        backward_kernel,
        [SEQUENCES, jax.ShapeDtypeStruct((CHANNELS, LENGTH), F32)],
        [GRID, TURNED, SECTION], 3,
        grad_owned, filter_spectrum, product_spectrum,
        first, first_back, cos_twist, sin_twist, second, second_back,
    )

    gated_all = lax.all_gather(gated, PLANE, axis=0).reshape(2, 4, rows, width)
    share = jnp.einsum("tymn,ynk->tmk", gated_all, weight, preferred_element_type=F32).astype(BF16)
    mine = jnp.where(half == 0, share[0], share[1])
    other = jnp.where(half == 0, share[1], share[0])
    mixed = (
        across(mine, lambda a, b: (b, a)).astype(F32)
        + across(other, lambda a, b: (1 - b, a)).astype(F32)
    ).astype(BF16)

    product_grad = lax.all_to_all(back_owned, SEQ, 0, 0, tiled=True).reshape(width, rows).T
    product_float = product_grad.astype(F32)
    grads = jnp.stack([query_conv_grad, product_float * value_conv, product_float * key_conv])
    after = shift(grads[:, :rim], -1)
    grads = jnp.concatenate([grads, after], axis=1)
    incoming = jnp.zeros(stacked.shape, F32)
    for tap in range(taps):
        incoming = incoming + short_taps[:, tap][:, None, :] * grads[:, tap : tap + rows]
    incoming = incoming.astype(BF16)
    return (mixed, incoming[0], incoming[1], incoming[2], filter_grad)


def solution(mesh):
    fine = Mesh(mesh.devices.reshape(2, 16, 2, 2, 4), ("xh", "z", "co", "xl", "y"))
    token = P(SEQ, TP)
    in_specs = (token, token, token, P(None, None, TP), P(TP + SEQ, None), token, token)
    out_specs = (token, token, token, token, P(TP + SEQ, None))
    return jax.shard_map(
        per_device, mesh=fine, in_specs=in_specs, out_specs=out_specs, check_vma=False
    )
```

```python
import functools
import math

import jax
import jax.numpy as jnp
import numpy as np
from jax import lax
from jax.experimental import pallas as pl
from jax.experimental.pallas import tpu as pltpu
from jax.sharding import Mesh
from jax.sharding import PartitionSpec as P

BF16 = jnp.bfloat16
F32 = jnp.float32

SEQ = ("xh", "z", "co")
TP = ("xl", "y")
PLANE = ("xh", "y")
COLUMN = ("z", "co")

CHANNELS = 16
BLOCKS = 64
LANES = 128
LENGTH = BLOCKS * LANES


def transform_tables():
    blocks = np.arange(BLOCKS)
    lanes = np.arange(LANES)
    first = 2.0 * np.pi * np.outer(blocks + 0.25, blocks) / BLOCKS
    twist = 2.0 * np.pi * np.outer(blocks + 0.25, lanes) / LENGTH
    second = 2.0 * np.pi * (np.outer(lanes, lanes) % LANES) / LANES
    first_table = np.concatenate([np.cos(first), -np.sin(first)], axis=0)
    cosine, sine = np.cos(second), np.sin(second)
    second_table = np.block([[cosine, -sine], [sine, cosine]])
    return (
        jnp.asarray(first_table, BF16),
        jnp.asarray(first_table.T / LENGTH, BF16),
        jnp.asarray(np.cos(twist), F32),
        jnp.asarray(np.sin(twist), F32),
        jnp.asarray(second_table, BF16),
        jnp.asarray(second_table.T, BF16),
    )


def to_spectrum(grid_ref, turned_ref, first, cos_twist, sin_twist, second):
    for c in range(CHANNELS):
        grid = grid_ref[pl.ds(c, BLOCKS, stride=CHANNELS), :].astype(BF16)
        section = jnp.dot(first, grid, preferred_element_type=F32)
        real, imag = section[:BLOCKS], section[BLOCKS:]
        rows = slice(c * BLOCKS, (c + 1) * BLOCKS)
        turned_ref[rows, :LANES] = (real * cos_twist + imag * sin_twist).astype(BF16)
        turned_ref[rows, LANES:] = (imag * cos_twist - real * sin_twist).astype(BF16)
    return jnp.dot(turned_ref[...], second, preferred_element_type=F32)


def from_spectrum(spectrum, grid_ref, section_ref, first_back, cos_twist, sin_twist, second_back):
    section_ref[...] = jnp.dot(spectrum, second_back, preferred_element_type=F32)
    for c in range(CHANNELS):
        rows = slice(c * BLOCKS, (c + 1) * BLOCKS)
        real, imag = section_ref[rows, :LANES], section_ref[rows, LANES:]
        turned = jnp.concatenate(
            [real * cos_twist - imag * sin_twist, imag * cos_twist + real * sin_twist], axis=0
        ).astype(BF16)
        grid_ref[pl.ds(c, BLOCKS, stride=CHANNELS), :] = jnp.dot(
            first_back, turned, preferred_element_type=F32
        )


def filter_kernel(filter_ref, first, cos_twist, sin_twist, second, spectrum_ref, grid, turned):
    for b in range(BLOCKS):
        grid[b * CHANNELS : (b + 1) * CHANNELS, :] = filter_ref[:, b * LANES : (b + 1) * LANES]
    spectrum_ref[...] = to_spectrum(
        grid, turned, first[...], cos_twist[...], sin_twist[...], second[...]
    )


def forward_kernel(
    product_ref, filter_spectrum, first, first_back, cos_twist, sin_twist, second, second_back,
    long_ref, product_spectrum, grid, turned, section,
):
    grid[...] = product_ref[...].astype(F32).reshape(BLOCKS * CHANNELS, LANES)
    own = to_spectrum(grid, turned, first[...], cos_twist[...], sin_twist[...], second[...])
    product_spectrum[...] = own
    own_re, own_im = own[:, :LANES], own[:, LANES:]
    other_re, other_im = filter_spectrum[:, :LANES], filter_spectrum[:, LANES:]
    turned[:, :LANES] = (own_re * other_re - own_im * other_im).astype(BF16)
    turned[:, LANES:] = (own_re * other_im + own_im * other_re).astype(BF16)
    from_spectrum(
        turned[...], grid, section, first_back[...], cos_twist[...], sin_twist[...], second_back[...]
    )
    long_ref[...] = grid[...].reshape(BLOCKS, CHANNELS, LANES).astype(BF16)


def backward_kernel(
    grad_ref, filter_spectrum, product_spectrum, _,
    first, first_back, cos_twist, sin_twist, second, second_back,
    back_ref, filter_grad_ref, grid, turned, section,
):
    grid[...] = grad_ref[...].astype(F32).reshape(BLOCKS * CHANNELS, LANES)
    own = to_spectrum(grid, turned, first[...], cos_twist[...], sin_twist[...], second[...])
    own_re, own_im = own[:, :LANES], own[:, LANES:]

    def correlate(other):
        other_re, other_im = other[:, :LANES], other[:, LANES:]
        turned[:, :LANES] = (own_re * other_re + own_im * other_im).astype(BF16)
        turned[:, LANES:] = (own_im * other_re - own_re * other_im).astype(BF16)
        from_spectrum(
            turned[...], grid, section, first_back[...], cos_twist[...], sin_twist[...], second_back[...]
        )

    correlate(filter_spectrum)
    back_ref[...] = grid[...].reshape(BLOCKS, CHANNELS, LANES).astype(BF16)
    correlate(product_spectrum)
    for b in range(BLOCKS):
        filter_grad_ref[:, b * LANES : (b + 1) * LANES] = grid[
            b * CHANNELS : (b + 1) * CHANNELS, :
        ] * (1.0 / math.sqrt(LENGTH))


SPECTRUM = jax.ShapeDtypeStruct((CHANNELS * BLOCKS, 2 * LANES), F32)
SEQUENCES = jax.ShapeDtypeStruct((BLOCKS, CHANNELS, LANES), BF16)
GRID = pltpu.VMEM((BLOCKS * CHANNELS, LANES), F32)
TURNED = pltpu.VMEM((CHANNELS * BLOCKS, 2 * LANES), BF16)
SECTION = pltpu.VMEM((CHANNELS * BLOCKS, 2 * LANES), F32)


def run_kernel(kernel, out_shape, scratch, transforms, *operands, unread=()):
    in_specs = [
        pl.BlockSpec(memory_space=pl.ANY if i in unread else pltpu.VMEM) for i in range(len(operands))
    ]
    transform_flops = 2 * CHANNELS * BLOCKS * LANES * (2 * BLOCKS + 4 * LANES)
    return pl.pallas_call(
        kernel,
        out_shape=out_shape,
        in_specs=in_specs,
        scratch_shapes=scratch,
        compiler_params=pltpu.CompilerParams(vmem_limit_bytes=40 * 2**20),
        cost_estimate=pl.CostEstimate(
            flops=transforms * transform_flops, bytes_accessed=4 * 2**20, transcendentals=0
        ),
    )(*operands)


def partial_kernel(gradient_ref, weight_ref, _, out_ref):
    rows = gradient_ref.shape[0] * gradient_ref.shape[1]
    product = lax.dot_general(
        gradient_ref[...].reshape(rows, -1), weight_ref[0], (((1,), (1,)), ((), ())),
        preferred_element_type=F32,
    )
    out_ref[...] = product.astype(BF16).reshape(out_ref.shape)


def partial_product(gradient, weight, after):
    halves, rows, features = gradient.shape
    groups, width, _ = weight.shape
    step = width // 2
    return pl.pallas_call(
        partial_kernel,
        grid=(groups, width // step),
        in_specs=[
            pl.BlockSpec((halves, rows, features), lambda y, n: (0, 0, 0)),
            pl.BlockSpec((1, step, features), lambda y, n: (y, n, 0)),
            pl.BlockSpec(memory_space=pl.ANY),
        ],
        out_specs=pl.BlockSpec((halves, 1, rows, step), lambda y, n: (0, y, 0, n)),
        out_shape=jax.ShapeDtypeStruct((halves, groups, rows, width), BF16),
        compiler_params=pltpu.CompilerParams(vmem_limit_bytes=24 * 2**20),
        cost_estimate=pl.CostEstimate(
            flops=2 * halves * rows * groups * width * features,
            bytes_accessed=8 * 2**20,
            transcendentals=0,
        ),
    )(gradient, weight, after)


def shift(value, steps):
    count = 1
    for axis in SEQ:
        count *= lax.axis_size(axis)
    first, last = max(0, -steps), min(count, count - steps)
    return lax.ppermute(value, SEQ, [(i, i + steps) for i in range(first, last)])


def across(value, target):
    pairs = [(2 * a + b, 2 * target(a, b)[0] + target(a, b)[1]) for a in range(2) for b in range(2)]
    return lax.ppermute(value, ("xh", "xl"), pairs)


def per_device(queries, keys, values, short_taps, long_filter, out_weight, cotangent):
    rows, width = queries.shape
    taps = short_taps.shape[1]
    rim = taps - 1
    features = out_weight.shape[1]
    half = lax.axis_index("xl")

    weight = lax.all_gather(
        across(out_weight, lambda a, b: (b, a)), COLUMN, axis=0, tiled=True
    ).reshape(4, width, features)
    near = across(cotangent, lambda a, b: (b, a))
    far = across(cotangent, lambda a, b: (b, 1 - a))
    gradient = jnp.where(half == 0, jnp.stack([near, far]), jnp.stack([far, near]))

    first, first_back, cos_twist, sin_twist, second, second_back = transform_tables()
    filter_spectrum = run_kernel(
        filter_kernel, SPECTRUM, [GRID, TURNED], 1, long_filter, first, cos_twist, sin_twist, second
    )

    stacked = jnp.stack([queries, keys, values])
    before = shift(stacked[:, rows - rim :], 1)
    extended = jnp.concatenate([before, stacked], axis=1).astype(F32)
    filtered = jnp.zeros(stacked.shape, F32)
    for tap in range(taps):
        start = rim - tap
        filtered = filtered + short_taps[:, tap][:, None, :] * extended[:, start : start + rows]
    query_conv, key_conv, value_conv = filtered[0], filtered[1], filtered[2]
    product = (key_conv * value_conv).astype(BF16)

    product_owned = lax.all_to_all(product.T.reshape(BLOCKS, CHANNELS, LANES), SEQ, 0, 0, tiled=True)
    long_owned, product_spectrum = run_kernel(
        forward_kernel, [SEQUENCES, SPECTRUM], [GRID, TURNED, SECTION], 2,
        product_owned, filter_spectrum, first, first_back, cos_twist, sin_twist, second, second_back,
    )
    long_out = lax.all_to_all(long_owned, SEQ, 0, 0, tiled=True).reshape(width, rows).T
    long_float = long_out.astype(F32)
    gated = (query_conv * long_float).astype(BF16)

    partial = partial_product(gradient, weight, gated).reshape(8, rows, width)
    gated_all = lax.all_gather(gated, PLANE, axis=0)
    gated_grad = jnp.sum(lax.all_to_all(partial, PLANE, 0, 0, tiled=True).astype(F32), axis=0)

    long_grad = (query_conv * gated_grad).astype(BF16)
    query_conv_grad = gated_grad * long_float
    grad_owned = lax.all_to_all(long_grad.T.reshape(BLOCKS, CHANNELS, LANES), SEQ, 0, 0, tiled=True)
    back_owned, filter_grad = run_kernel(
        backward_kernel,
        [SEQUENCES, jax.ShapeDtypeStruct((CHANNELS, LENGTH), F32)],
        [GRID, TURNED, SECTION], 3,
        grad_owned, filter_spectrum, product_spectrum, gated_all,
        first, first_back, cos_twist, sin_twist, second, second_back, unread=(3,),
    )

    gated_all = gated_all.reshape(2, 4, rows, width)
    share = jnp.einsum("tymn,ynk->tmk", gated_all, weight, preferred_element_type=F32).astype(BF16)
    mine = jnp.where(half == 0, share[0], share[1])
    other = jnp.where(half == 0, share[1], share[0])
    mixed = (
        across(mine, lambda a, b: (b, a)).astype(F32)
        + across(other, lambda a, b: (1 - b, a)).astype(F32)
    ).astype(BF16)

    product_grad = lax.all_to_all(back_owned, SEQ, 0, 0, tiled=True).reshape(width, rows).T
    product_float = product_grad.astype(F32)
    grads = jnp.stack([query_conv_grad, product_float * value_conv, product_float * key_conv])
    after = shift(grads[:, :rim], -1)
    grads = jnp.concatenate([grads, after], axis=1)
    incoming = jnp.zeros(stacked.shape, F32)
    for tap in range(taps):
        incoming = incoming + short_taps[:, tap][:, None, :] * grads[:, tap : tap + rows]
    incoming = incoming.astype(BF16)
    return (mixed, incoming[0], incoming[1], incoming[2], filter_grad)


def solution(mesh):
    fine = Mesh(mesh.devices.reshape(2, 16, 2, 2, 4), ("xh", "z", "co", "xl", "y"))
    token = P(SEQ, TP)
    in_specs = (token, token, token, P(None, None, TP), P(TP + SEQ, None), token, token)
    out_specs = (token, token, token, token, P(TP + SEQ, None))
    return jax.shard_map(
        per_device, mesh=fine, in_specs=in_specs, out_specs=out_specs, check_vma=False
    )
```

```python
import math

import jax
import jax.numpy as jnp
import numpy as np
from jax import lax
from jax.experimental import pallas as pl
from jax.experimental.pallas import tpu as pltpu
from jax.sharding import Mesh
from jax.sharding import PartitionSpec as P

BF16 = jnp.bfloat16
F32 = jnp.float32

SEQ = ("xh", "z", "co")
TP = ("xl", "y")
ROW = ("xh", "xl")
PLANE = ("xh", "y")
COLUMN = ("z", "co")

CHANNELS = 16
BLOCKS = 64
LANES = 128
LENGTH = BLOCKS * LANES


def transform_tables():
    blocks = np.arange(BLOCKS)
    lanes = np.arange(LANES)
    first = 2.0 * np.pi * np.outer(blocks + 0.25, blocks) / BLOCKS
    twist = 2.0 * np.pi * np.outer(blocks + 0.25, lanes) / LENGTH
    second = 2.0 * np.pi * (np.outer(lanes, lanes) % LANES) / LANES
    first_table = np.concatenate([np.cos(first), -np.sin(first)], axis=0)
    cosine, sine = np.cos(second), np.sin(second)
    second_table = np.block([[cosine, -sine], [sine, cosine]])
    steps = np.zeros((2 * LANES, 5 * LANES))
    steps[:, : 2 * LANES] = second_table
    steps[:, 2 * LANES : 4 * LANES] = second_table.T
    steps[: 2 * BLOCKS, 4 * LANES : 4 * LANES + BLOCKS] = first_table
    steps[2 * BLOCKS : 3 * BLOCKS, 4 * LANES : 4 * LANES + 2 * BLOCKS] = first_table.T / LENGTH
    turns = np.concatenate([np.cos(twist), np.sin(twist)], axis=1)
    return jnp.asarray(steps, BF16), jnp.asarray(turns, F32)


def to_spectrum(grid_ref, turned_ref, steps, turns):
    first = steps[: 2 * BLOCKS, 4 * LANES : 4 * LANES + BLOCKS]
    cos_twist, sin_twist = turns[:, :LANES], turns[:, LANES:]
    for c in range(CHANNELS):
        grid = grid_ref[pl.ds(c, BLOCKS, stride=CHANNELS), :].astype(BF16)
        section = jnp.dot(first, grid, preferred_element_type=F32)
        real, imag = section[:BLOCKS], section[BLOCKS:]
        rows = slice(c * BLOCKS, (c + 1) * BLOCKS)
        turned_ref[rows, :LANES] = (real * cos_twist + imag * sin_twist).astype(BF16)
        turned_ref[rows, LANES:] = (imag * cos_twist - real * sin_twist).astype(BF16)
    return jnp.dot(turned_ref[...], steps[:, : 2 * LANES], preferred_element_type=F32)


def from_spectrum(spectrum, grid_ref, section_ref, steps, turns):
    first_back = steps[2 * BLOCKS : 3 * BLOCKS, 4 * LANES : 4 * LANES + 2 * BLOCKS]
    cos_twist, sin_twist = turns[:, :LANES], turns[:, LANES:]
    section_ref[...] = jnp.dot(
        spectrum, steps[:, 2 * LANES : 4 * LANES], preferred_element_type=F32
    )
    for c in range(CHANNELS):
        rows = slice(c * BLOCKS, (c + 1) * BLOCKS)
        real, imag = section_ref[rows, :LANES], section_ref[rows, LANES:]
        turned = jnp.concatenate(
            [real * cos_twist - imag * sin_twist, imag * cos_twist + real * sin_twist], axis=0
        ).astype(BF16)
        grid_ref[pl.ds(c, BLOCKS, stride=CHANNELS), :] = jnp.dot(
            first_back, turned, preferred_element_type=F32
        )


def filter_kernel(filter_ref, steps, turns, spectrum_ref, grid, turned):
    for b in range(BLOCKS):
        grid[b * CHANNELS : (b + 1) * CHANNELS, :] = filter_ref[:, b * LANES : (b + 1) * LANES]
    spectrum_ref[...] = to_spectrum(grid, turned, steps, turns)


def forward_kernel(
    product_ref, filter_spectrum, steps, turns, long_ref, product_spectrum, grid, turned, section
):
    grid[...] = product_ref[...].astype(F32).reshape(BLOCKS * CHANNELS, LANES)
    own = to_spectrum(grid, turned, steps, turns)
    product_spectrum[...] = own
    own_re, own_im = own[:, :LANES], own[:, LANES:]
    other_re, other_im = filter_spectrum[:, :LANES], filter_spectrum[:, LANES:]
    turned[:, :LANES] = (own_re * other_re - own_im * other_im).astype(BF16)
    turned[:, LANES:] = (own_re * other_im + own_im * other_re).astype(BF16)
    from_spectrum(turned[...], grid, section, steps, turns)
    long_ref[...] = grid[...].reshape(BLOCKS, CHANNELS, LANES).astype(BF16)


def backward_kernel(
    grad_ref, filter_spectrum, product_spectrum, _, steps, turns,
    back_ref, filter_grad_ref, grid, turned, section,
):
    grid[...] = grad_ref[...].astype(F32).reshape(BLOCKS * CHANNELS, LANES)
    own = to_spectrum(grid, turned, steps, turns)
    own_re, own_im = own[:, :LANES], own[:, LANES:]

    def correlate(other):
        other_re, other_im = other[:, :LANES], other[:, LANES:]
        turned[:, :LANES] = (own_re * other_re + own_im * other_im).astype(BF16)
        turned[:, LANES:] = (own_im * other_re - own_re * other_im).astype(BF16)
        from_spectrum(turned[...], grid, section, steps, turns)

    correlate(filter_spectrum)
    back_ref[...] = grid[...].reshape(BLOCKS, CHANNELS, LANES).astype(BF16)
    correlate(product_spectrum)
    for b in range(BLOCKS):
        filter_grad_ref[:, b * LANES : (b + 1) * LANES] = grid[
            b * CHANNELS : (b + 1) * CHANNELS, :
        ] * (1.0 / math.sqrt(LENGTH))


SPECTRUM = jax.ShapeDtypeStruct((CHANNELS * BLOCKS, 2 * LANES), F32)
SEQUENCES = jax.ShapeDtypeStruct((BLOCKS, CHANNELS, LANES), BF16)
GRID = pltpu.VMEM((BLOCKS * CHANNELS, LANES), F32)
TURNED = pltpu.VMEM((CHANNELS * BLOCKS, 2 * LANES), BF16)
SECTION = pltpu.VMEM((CHANNELS * BLOCKS, 2 * LANES), F32)


def run_kernel(kernel, out_shape, scratch, transforms, *operands, unread=()):
    in_specs = [
        pl.BlockSpec(memory_space=pl.ANY if i in unread else pltpu.VMEM) for i in range(len(operands))
    ]
    transform_flops = 2 * CHANNELS * BLOCKS * LANES * (2 * BLOCKS + 4 * LANES)
    return pl.pallas_call(
        kernel,
        out_shape=out_shape,
        in_specs=in_specs,
        scratch_shapes=scratch,
        compiler_params=pltpu.CompilerParams(vmem_limit_bytes=20 * 2**20),
        cost_estimate=pl.CostEstimate(
            flops=transforms * transform_flops, bytes_accessed=4 * 2**20, transcendentals=0
        ),
    )(*operands)


def run_blocks(kernel, steps, ins, outs, moved, flops=10**6, scratch=()):
    def spec(block, axis):
        if block is None:
            return pl.BlockSpec(memory_space=pl.ANY)
        return pl.BlockSpec(block, lambda i: tuple(i if d == axis else 0 for d in range(len(block))))

    return pl.pallas_call(
        kernel,
        grid=(steps,),
        in_specs=[spec(block, axis) for _, block, axis in ins],
        out_specs=[spec(block, axis) for _, _, block, axis in outs],
        out_shape=[jax.ShapeDtypeStruct(shape, dtype) for shape, dtype, _, _ in outs],
        scratch_shapes=list(scratch),
        compiler_params=pltpu.CompilerParams(vmem_limit_bytes=20 * 2**20),
        cost_estimate=pl.CostEstimate(flops=flops, bytes_accessed=moved, transcendentals=0),
    )(*[array for array, _, _ in ins])


def row_numbers(value):
    return lax.broadcasted_iota(jnp.int32, value.shape, 0)


def causal(value, before, taps):
    number = row_numbers(value)
    one = jnp.where(number == 0, before[1:2], pltpu.roll(value, 1, 0))
    two = jnp.where(number == 0, before[0:1], pltpu.roll(value, 2, 0))
    two = jnp.where(number == 1, before[1:2], two)
    return taps[0:1] * value + taps[1:2] * one + taps[2:3] * two


def adjoint(value, after, taps):
    rows = value.shape[0]
    number = row_numbers(value)
    one = jnp.where(number == rows - 1, after[0:1], pltpu.roll(value, rows - 1, 0))
    two = jnp.where(number == rows - 1, after[1:2], pltpu.roll(value, rows - 2, 0))
    two = jnp.where(number == rows - 2, after[0:1], two)
    return taps[0:1] * value + taps[1:2] * one + taps[2:3] * two


def filter_inputs(q_ref, k_ref, v_ref, before_ref, taps_ref, qc_ref, kc_ref, vc_ref, product_ref):
    sources = (q_ref, k_ref, v_ref)
    qc, kc, vc = (
        causal(sources[i][...].astype(F32), before_ref[i].astype(F32), taps_ref[i]) for i in range(3)
    )
    qc_ref[...], kc_ref[...], vc_ref[...] = qc, kc, vc
    product_ref[...] = (kc * vc).T.astype(BF16)


def gate(long_ref, qc_ref, out_ref, gated_ref):
    long = long_ref[...].astype(F32).T
    out_ref[...] = long
    gated = (qc_ref[...] * long).astype(BF16)
    gated_ref[0] = gated[:, :LANES]
    gated_ref[1] = gated[:, LANES:]


def partial_kernel(gradient_ref, weight_ref, _, out_ref):
    halves, groups, rows, features = gradient_ref.shape
    width = weight_ref.shape[0] * weight_ref.shape[2]
    total = jnp.zeros((halves * rows, width), F32)
    for f in range(groups):
        total += lax.dot_general(
            gradient_ref[:, f].reshape(halves * rows, features),
            weight_ref[:, f].reshape(width, features),
            (((1,), (1,)), ((), ())),
            preferred_element_type=F32,
        )
    out_ref[...] = total.astype(BF16).reshape(out_ref.shape)


def long_gradient(parts_ref, qc_ref, long_ref, grad_ref, qg_ref):
    parts = parts_ref[...].astype(F32)
    gated_grad = jnp.concatenate(
        [(parts[r] + parts[r + 1]) + (parts[r + 2] + parts[r + 3]) for r in (0, 4)], axis=1
    )
    grad_ref[...] = (qc_ref[...] * gated_grad).T.astype(BF16)
    qg_ref[...] = gated_grad * long_ref[...]


def mix_kernel(gated_ref, weight_ref, out_ref, total):
    halves, rows, width = gated_ref.shape[1:]
    groups, features = weight_ref.shape[1], weight_ref.shape[3]
    step = pl.program_id(0)

    @pl.when(step == 0)
    def _():
        total[...] = jnp.zeros_like(total)

    gated = gated_ref[...].reshape(halves * rows, width)
    for f in range(groups):
        total[f] += jnp.dot(
            gated, weight_ref[:, f].reshape(width, features), preferred_element_type=F32
        )

    @pl.when(step == pl.num_programs(0) - 1)
    def _():
        out_ref[...] = total[...].astype(BF16).reshape(out_ref.shape)


def query_adjoint(qg_ref, after_ref, taps_ref, out_ref):
    out_ref[...] = adjoint(qg_ref[...], after_ref[...], taps_ref[0]).astype(BF16)


def key_value_adjoint(
    back_ref, kc_ref, vc_ref, after_ref, next_ref, taps_ref, key_ref, value_ref
):
    back = back_ref[...].astype(F32).T
    after = after_ref[...].astype(F32)
    key_ref[...] = adjoint(back * vc_ref[...], after * next_ref[1], taps_ref[1]).astype(BF16)
    value_ref[...] = adjoint(back * kc_ref[...], after * next_ref[0], taps_ref[2]).astype(BF16)


def shift(value, steps):
    count = 1
    for axis in SEQ:
        count *= lax.axis_size(axis)
    first, last = max(0, -steps), min(count, count - steps)
    return lax.ppermute(value, SEQ, [(i, i + steps) for i in range(first, last)])


def across(value, dx, dl):
    if not (dx or dl):
        return value
    return lax.ppermute(value, ROW, [(i, i ^ (2 * dx + dl)) for i in range(4)])


def per_device(queries, keys, values, short_taps, long_filter, out_weight, cotangent):
    rows, width = queries.shape
    features = out_weight.shape[1]
    own_xh, own_xl = lax.axis_index("xh"), lax.axis_index("xl")
    kinds, chunk = 4, width // 4

    turned = lax.ppermute(
        out_weight,
        ("xh", "co", "xl"),
        [(4 * a + 2 * c + b, 4 * c + 2 * b + a) for a in range(2) for c in range(2) for b in range(2)],
    )
    weight = lax.all_gather(turned, COLUMN, axis=0).reshape(16, 2, rows, features)

    before = shift(jnp.stack([x[rows - 2 :] for x in (queries, keys, values)]), 1)
    steps, turns = transform_tables()
    filter_spectrum = run_kernel(filter_kernel, SPECTRUM, [GRID, TURNED], 1, long_filter, steps, turns)

    tokens = (rows, chunk)
    channels = (chunk, rows)
    taps_block = (3, 3, chunk)
    plane = ((rows, width), F32, tokens, 1)
    query_conv, key_conv, value_conv, product = run_blocks(
        filter_inputs, kinds,
        [(queries, tokens, 1), (keys, tokens, 1), (values, tokens, 1),
         (before, (3, 2, chunk), 2), (short_taps, taps_block, 2)],
        [plane, plane, plane, ((width, rows), BF16, channels, 0)], 3 * 2**20,
    )

    product_owned = lax.all_to_all(product.reshape(BLOCKS, CHANNELS, LANES), SEQ, 0, 0, tiled=True)
    long_owned, product_spectrum = run_kernel(
        forward_kernel, [SEQUENCES, SPECTRUM], [GRID, TURNED, SECTION], 2,
        product_owned, filter_spectrum, steps, turns,
    )
    blocks = [[across(cotangent, dx, dl) for dl in range(2)] for dx in range(2)]
    gradient = jnp.stack([jnp.stack(line) for line in blocks])
    gradient = jnp.where(own_xh == 0, gradient, gradient[::-1])
    gradient = jnp.where(own_xl == 0, gradient, gradient[:, ::-1])

    long_raw = lax.all_to_all(long_owned, SEQ, 0, 0, tiled=True).reshape(width, rows)
    long_out, gated = run_blocks(
        gate, kinds,
        [(long_raw, channels, 0), (query_conv, tokens, 1)],
        [plane, ((2, rows, width // 2), BF16, (2, rows, LANES), 2)], 2 * 2**20,
    )

    quarter = (4, 2, rows, features)
    (partial,) = run_blocks(
        partial_kernel, kinds,
        [(gradient, gradient.shape, None), (weight, quarter, 0), (gated, None, None)],
        [((2, 4, rows, width // 2), BF16, (2, 1, rows, width // 2), 1)], 6 * 2**20, 2**30,
    )
    parts = lax.all_to_all(partial.reshape(8, rows, width // 2), PLANE, 0, 0, tiled=True)
    long_grad, query_conv_grad = run_blocks(
        long_gradient, kinds,
        [(parts, (8, rows, LANES), 2), (query_conv, tokens, 1), (long_out, tokens, 1)],
        [((width, rows), BF16, channels, 0), plane], 3 * 2**20,
    )
    grad_owned = lax.all_to_all(long_grad.reshape(BLOCKS, CHANNELS, LANES), SEQ, 0, 0, tiled=True)

    keep = jnp.where(own_xh == 0, gated[0], gated[1])
    send = jnp.where(own_xh == 0, gated[1], gated[0])
    gated_all = lax.all_gather(jnp.stack([keep, across(send, 1, 0)]), "y", axis=0)

    back_owned, filter_grad = run_kernel(
        backward_kernel,
        [SEQUENCES, jax.ShapeDtypeStruct((CHANNELS, LENGTH), F32)],
        [GRID, TURNED, SECTION], 3,
        grad_owned, filter_spectrum, product_spectrum, gated_all, steps, turns, unread=(3,),
    )

    (share,) = run_blocks(
        mix_kernel, kinds,
        [(gated_all, (1, 2, rows, width // 2), 0), (weight, quarter, 0)],
        [((2, 2, rows, features), BF16, (2, 2, rows, features), None)], 6 * 2**20, 2**30,
        [pltpu.VMEM((2, 2 * rows, features), F32)],
    )
    share = jnp.where(own_xl == 0, share, share[::-1])
    mixed = share[0, 0].astype(F32)
    for dx, dl in ((0, 1), (1, 0), (1, 1)):
        mixed = mixed + across(share[dl, dx], dx, dl).astype(F32)
    mixed = mixed.astype(BF16)

    rim = (2, chunk)
    (query_grad,) = run_blocks(
        query_adjoint, kinds,
        [(query_conv_grad, tokens, 1), (shift(query_conv_grad[:2], -1), rim, 1), (short_taps, taps_block, 2)],
        [((rows, width), BF16, tokens, 1)], 2**20,
    )
    following = shift(jnp.stack([key_conv[:2], value_conv[:2]]), -1)

    back_raw = lax.all_to_all(back_owned, SEQ, 0, 0, tiled=True).reshape(width, rows)
    after = shift(back_raw[:, :2].T, -1)
    key_grad, value_grad = run_blocks(
        key_value_adjoint, kinds,
        [(back_raw, channels, 0), (key_conv, tokens, 1), (value_conv, tokens, 1),
         (after, rim, 1), (following, (2, 2, chunk), 2), (short_taps, taps_block, 2)],
        [((rows, width), BF16, tokens, 1)] * 2, 3 * 2**20,
    )
    return (mixed, query_grad, key_grad, value_grad, filter_grad)


def solution(mesh):
    fine = Mesh(mesh.devices.reshape(2, 16, 2, 2, 4), ("xh", "z", "co", "xl", "y"))
    token = P(SEQ, TP)
    in_specs = (token, token, token, P(None, None, TP), P(TP + SEQ, None), token, token)
    out_specs = (token, token, token, token, P(TP + SEQ, None))
    return jax.shard_map(
        per_device, mesh=fine, in_specs=in_specs, out_specs=out_specs, check_vma=False
    )
```

```python
import math

import jax
import jax.numpy as jnp
import numpy as np
from jax import lax
from jax.experimental import pallas as pl
from jax.experimental.pallas import tpu as pltpu
from jax.sharding import Mesh
from jax.sharding import PartitionSpec as P

BF16 = jnp.bfloat16
F32 = jnp.float32

AXES = {"xh": 2, "zy": 4, "zh": 2, "zb": 2, "co": 2, "xl": 2, "yh": 2, "yl": 2}
SEQ = ("xh", "zy", "zh", "zb", "co")
TP = ("xl", "yh", "yl")
PLANE = ("xh", "yh", "yl")
COLUMN = ("zy", "zh", "zb", "co")

CHANNELS = 16
BLOCKS = 64
LANES = 128
LENGTH = BLOCKS * LANES

VMEM_LIMIT = 20 * 2**20
WHOLE_VMEM = 60 * 2**20


def transform_tables():
    blocks = np.arange(BLOCKS)
    lanes = np.arange(LANES)
    first = 2.0 * np.pi * np.outer(blocks + 0.25, blocks) / BLOCKS
    twist = 2.0 * np.pi * np.outer(blocks + 0.25, lanes) / LENGTH
    second = 2.0 * np.pi * (np.outer(lanes, lanes) % LANES) / LANES
    first_table = np.concatenate([np.cos(first), -np.sin(first)], axis=0)
    cosine, sine = np.cos(second), np.sin(second)
    second_table = np.block([[cosine, -sine], [sine, cosine]])
    steps = np.zeros((2 * LANES, 5 * LANES))
    steps[:, : 2 * LANES] = second_table
    steps[:, 2 * LANES : 4 * LANES] = second_table.T
    steps[: 2 * BLOCKS, 4 * LANES : 4 * LANES + BLOCKS] = first_table
    steps[2 * BLOCKS : 3 * BLOCKS, 4 * LANES : 4 * LANES + 2 * BLOCKS] = first_table.T / LENGTH
    turns = np.concatenate([np.cos(twist), np.sin(twist)], axis=1)
    return jnp.asarray(steps, BF16), jnp.asarray(turns, F32)


def to_spectrum(grid_ref, turned_ref, steps, turns):
    first = steps[: 2 * BLOCKS, 4 * LANES : 4 * LANES + BLOCKS]
    cos_twist, sin_twist = turns[:, :LANES], turns[:, LANES:]
    for c in range(CHANNELS):
        grid = grid_ref[pl.ds(c, BLOCKS, stride=CHANNELS), :].astype(BF16)
        section = jnp.dot(first, grid, preferred_element_type=F32)
        real, imag = section[:BLOCKS], section[BLOCKS:]
        rows = slice(c * BLOCKS, (c + 1) * BLOCKS)
        turned_ref[rows, :LANES] = (real * cos_twist + imag * sin_twist).astype(BF16)
        turned_ref[rows, LANES:] = (imag * cos_twist - real * sin_twist).astype(BF16)
    return jnp.dot(turned_ref[...], steps[:, : 2 * LANES], preferred_element_type=F32)


def from_spectrum(spectrum, grid_ref, section_ref, steps, turns):
    first_back = steps[2 * BLOCKS : 3 * BLOCKS, 4 * LANES : 4 * LANES + 2 * BLOCKS]
    cos_twist, sin_twist = turns[:, :LANES], turns[:, LANES:]
    section_ref[...] = jnp.dot(
        spectrum, steps[:, 2 * LANES : 4 * LANES], preferred_element_type=F32
    )
    for c in range(CHANNELS):
        rows = slice(c * BLOCKS, (c + 1) * BLOCKS)
        real, imag = section_ref[rows, :LANES], section_ref[rows, LANES:]
        turned = jnp.concatenate(
            [real * cos_twist - imag * sin_twist, imag * cos_twist + real * sin_twist], axis=0
        ).astype(BF16)
        grid_ref[pl.ds(c, BLOCKS, stride=CHANNELS), :] = jnp.dot(
            first_back, turned, preferred_element_type=F32
        )


def filter_kernel(filter_ref, steps, turns, spectrum_ref, grid, turned):
    for b in range(BLOCKS):
        grid[b * CHANNELS : (b + 1) * CHANNELS, :] = filter_ref[:, b * LANES : (b + 1) * LANES]
    spectrum_ref[...] = to_spectrum(grid, turned, steps, turns)


def forward_kernel(
    product_ref, filter_spectrum, steps, turns, long_ref, product_spectrum, grid, turned, section
):
    grid[...] = product_ref[...].astype(F32).reshape(BLOCKS * CHANNELS, LANES)
    own = to_spectrum(grid, turned, steps, turns)
    product_spectrum[...] = own
    own_re, own_im = own[:, :LANES], own[:, LANES:]
    other_re, other_im = filter_spectrum[:, :LANES], filter_spectrum[:, LANES:]
    turned[:, :LANES] = (own_re * other_re - own_im * other_im).astype(BF16)
    turned[:, LANES:] = (own_re * other_im + own_im * other_re).astype(BF16)
    from_spectrum(turned[...], grid, section, steps, turns)
    long_ref[...] = grid[...].reshape(BLOCKS, CHANNELS, LANES).astype(BF16)


def backward_kernel(
    grad_ref, filter_spectrum, product_spectrum, steps, turns,
    back_ref, filter_grad_ref, grid, turned, section,
):
    grid[...] = grad_ref[...].astype(F32).reshape(BLOCKS * CHANNELS, LANES)
    own = to_spectrum(grid, turned, steps, turns)
    own_re, own_im = own[:, :LANES], own[:, LANES:]

    def correlate(other):
        other_re, other_im = other[:, :LANES], other[:, LANES:]
        turned[:, :LANES] = (own_re * other_re + own_im * other_im).astype(BF16)
        turned[:, LANES:] = (own_im * other_re - own_re * other_im).astype(BF16)
        from_spectrum(turned[...], grid, section, steps, turns)

    correlate(filter_spectrum)
    back_ref[...] = grid[...].reshape(BLOCKS, CHANNELS, LANES).astype(BF16)
    correlate(product_spectrum)
    for b in range(BLOCKS):
        filter_grad_ref[:, b * LANES : (b + 1) * LANES] = grid[
            b * CHANNELS : (b + 1) * CHANNELS, :
        ] * (1.0 / math.sqrt(LENGTH))


SPECTRUM = jax.ShapeDtypeStruct((CHANNELS * BLOCKS, 2 * LANES), F32)
SEQUENCES = jax.ShapeDtypeStruct((BLOCKS, CHANNELS, LANES), BF16)
GRID = pltpu.VMEM((BLOCKS * CHANNELS, LANES), F32)
TURNED = pltpu.VMEM((CHANNELS * BLOCKS, 2 * LANES), BF16)
SECTION = pltpu.VMEM((CHANNELS * BLOCKS, 2 * LANES), F32)


def run_kernel(kernel, out_shape, scratch, transforms, *operands, unread=()):
    in_specs = [
        pl.BlockSpec(memory_space=pl.ANY if i in unread else pltpu.VMEM) for i in range(len(operands))
    ]
    transform_flops = 2 * CHANNELS * BLOCKS * LANES * (2 * BLOCKS + 4 * LANES)
    return pl.pallas_call(
        kernel,
        out_shape=out_shape,
        in_specs=in_specs,
        scratch_shapes=scratch,
        compiler_params=pltpu.CompilerParams(vmem_limit_bytes=VMEM_LIMIT),
        cost_estimate=pl.CostEstimate(
            flops=transforms * transform_flops, bytes_accessed=4 * 2**20, transcendentals=0
        ),
    )(*operands)


def run_blocks(kernel, steps, ins, outs, moved, flops=10**6, scratch=(), limit=VMEM_LIMIT):
    def spec(block, axis):
        if block is None:
            return pl.BlockSpec(memory_space=axis or pl.ANY)
        fixed = (0,) * len(block)
        if isinstance(block[0], tuple):
            block, fixed = block[0], (0,) * (len(block[0]) - 3) + (block[1][1],) + (0, 0)
        return pl.BlockSpec(block, lambda i: tuple(i if d == axis else fixed[d] for d in range(len(block))))

    return pl.pallas_call(
        kernel,
        grid=(steps,),
        in_specs=[spec(block, axis) for _, block, axis in ins],
        out_specs=[spec(block, axis) for _, _, block, axis in outs],
        out_shape=[jax.ShapeDtypeStruct(shape, dtype) for shape, dtype, _, _ in outs],
        scratch_shapes=list(scratch),
        compiler_params=pltpu.CompilerParams(vmem_limit_bytes=limit),
        cost_estimate=pl.CostEstimate(flops=flops, bytes_accessed=moved, transcendentals=0),
    )(*[array for array, _, _ in ins])


def row_numbers(value):
    return lax.broadcasted_iota(jnp.int32, value.shape, 0)


def causal(value, before, taps):
    number = row_numbers(value)
    one = jnp.where(number == 0, before[1:2], pltpu.roll(value, 1, 0))
    two = jnp.where(number == 0, before[0:1], pltpu.roll(value, 2, 0))
    two = jnp.where(number == 1, before[1:2], two)
    return taps[0:1] * value + taps[1:2] * one + taps[2:3] * two


def adjoint(value, after, taps):
    rows = value.shape[0]
    number = row_numbers(value)
    one = jnp.where(number == rows - 1, after[0:1], pltpu.roll(value, rows - 1, 0))
    two = jnp.where(number == rows - 1, after[1:2], pltpu.roll(value, rows - 2, 0))
    two = jnp.where(number == rows - 2, after[0:1], two)
    return taps[0:1] * value + taps[1:2] * one + taps[2:3] * two


def filter_inputs(q_ref, k_ref, v_ref, before_ref, taps_ref, qc_ref, kc_ref, vc_ref, product_ref):
    sources = (q_ref, k_ref, v_ref)
    qc, kc, vc = (
        causal(sources[i][...].astype(F32), before_ref[i].astype(F32), taps_ref[i]) for i in range(3)
    )
    qc_ref[...], kc_ref[...], vc_ref[...] = qc, kc, vc
    product_ref[...] = (kc * vc).T.astype(BF16)


def gate(long_ref, qc_ref, out_ref, gated_ref):
    long = long_ref[...].astype(F32).T
    out_ref[...] = long
    gated = (qc_ref[...] * long).astype(BF16)
    for zb in range(2):
        for co in range(2):
            start = (2 * zb + co) * LANES
            gated_ref[co, zb] = gated[:, start : start + LANES]


def partial_kernel(place_ref, gradient_ref, weight_ref, gated_ref, out_ref):
    xh, xl, yl = place_ref[0], place_ref[1], place_ref[3]
    rows, features = gradient_ref.shape[3:]
    width = out_ref.shape[4]
    total = jnp.zeros((2 * rows, width), F32)
    for e in range(2):
        for f in range(2):
            total += lax.dot_general(
                gradient_ref[e ^ yl, f ^ xl].reshape(2 * rows, features),
                weight_ref[0, :, e, f].reshape(width, features),
                (((1,), (1,)), ((), ())),
                preferred_element_type=F32,
            )
    for t in range(2):
        out_ref[t ^ xh, 0, 0] = total[t * rows : (t + 1) * rows].astype(BF16)
        out_ref[t, 0, 1] = gated_ref[t, pl.program_id(0) % 2]


def long_gradient(parts_ref, qc_ref, long_ref, grad_ref, qg_ref):
    parts = parts_ref[...].astype(F32).reshape(8, *qg_ref.shape[:1], LANES)
    gated_grad = jnp.concatenate(
        [parts[4 * r + e] + parts[4 * r + 2 + e] for e in range(2) for r in range(2)], axis=1
    )
    grad_ref[...] = (qc_ref[...] * gated_grad).T.astype(BF16)
    qg_ref[...] = gated_grad * long_ref[...]


def mix_kernel(gated_ref, weight_ref, out_ref, total):
    halves, _, _, rows, width = gated_ref.shape
    features = weight_ref.shape[5]
    step = pl.program_id(0)

    @pl.when(step == 0)
    def _():
        total[...] = jnp.zeros_like(total)

    gated = gated_ref[...].reshape(halves * rows, width)
    for e in range(2):
        for f in range(2):
            total[2 * e + f] += jnp.dot(
                gated, weight_ref[0, :, e, f].reshape(width, features), preferred_element_type=F32
            )

    @pl.when(step == pl.num_programs(0) - 1)
    def _():
        for e in range(2):
            for f in range(2):
                for t in range(2):
                    out_ref[t, f, e] = total[2 * e + f, t * rows : (t + 1) * rows].astype(BF16)


def query_adjoint(qg_ref, after_ref, taps_ref, out_ref):
    out_ref[...] = adjoint(qg_ref[...], after_ref[...], taps_ref[0]).astype(BF16)


def key_value_adjoint(
    back_ref, kc_ref, vc_ref, after_ref, next_ref, taps_ref, key_ref, value_ref
):
    back = back_ref[...].astype(F32).T
    after = after_ref[...].astype(F32)
    key_ref[...] = adjoint(back * vc_ref[...], after * next_ref[1], taps_ref[1]).astype(BF16)
    value_ref[...] = adjoint(back * kc_ref[...], after * next_ref[0], taps_ref[2]).astype(BF16)


def shift(value, steps):
    count = 1
    for axis in SEQ:
        count *= lax.axis_size(axis)
    first, last = max(0, -steps), min(count, count - steps)
    return lax.ppermute(value, SEQ, [(i, i + steps) for i in range(first, last)])


def partner(value, axis):
    return lax.ppermute(value, axis, [(0, 1), (1, 0)])


def across(value, dx, dl):
    if not (dx or dl):
        return value
    return lax.ppermute(value, ("xh", "xl"), [(i, i ^ (2 * dx + dl)) for i in range(4)])


def turn(value):
    pairs = []
    for i in range(32):
        a, s, c, b, e = ((i >> k) & 1 for k in (4, 3, 2, 1, 0))
        pairs.append((i, 16 * c + 8 * e + 4 * b + 2 * a + s))
    return lax.ppermute(value, ("xh", "zb", "co", "xl", "yl"), pairs)


def per_device(queries, keys, values, short_taps, long_filter, out_weight, cotangent):
    rows, width = queries.shape
    features = out_weight.shape[1]
    place = jnp.stack([lax.axis_index(axis) for axis in ("xh", "xl", "yh", "yl")])
    place = (place.astype(jnp.int32), None, pltpu.SMEM)
    kinds, chunk = 4, width // 4

    rims = jnp.stack([x[rows - 2 :] for x in (queries, keys, values)])
    rims, out_weight = lax.optimization_barrier((rims, out_weight))
    before, turned = lax.optimization_barrier((shift(rims, 1), turn(out_weight)))
    weight = lax.all_gather(turned, COLUMN, axis=0).reshape(4, 2, 2, 2, rows, features)
    weight = pltpu.with_memory_space_constraint(weight, pltpu.HBM)

    steps, turns = transform_tables()
    filter_spectrum = run_kernel(filter_kernel, SPECTRUM, [GRID, TURNED], 1, long_filter, steps, turns)

    tokens = (rows, chunk)
    channels = (chunk, rows)
    taps_block = (3, 3, chunk)
    plane = ((rows, width), F32, tokens, 1)
    query_conv, key_conv, value_conv, product = run_blocks(
        filter_inputs, kinds,
        [(queries, tokens, 1), (keys, tokens, 1), (values, tokens, 1),
         (before, (3, 2, chunk), 2), (short_taps, taps_block, 2)],
        [plane, plane, plane, ((width, rows), BF16, channels, 0)], 3 * 2**20, limit=WHOLE_VMEM,
    )

    product_owned = lax.all_to_all(product.reshape(BLOCKS, CHANNELS, LANES), SEQ, 0, 0, tiled=True)
    long_owned, product_spectrum = run_kernel(
        forward_kernel, [SEQUENCES, SPECTRUM], [GRID, TURNED, SECTION], 2,
        product_owned, filter_spectrum, steps, turns,
    )
    gradient = jnp.stack([jnp.stack([across(cotangent, dx, dl) for dx in range(2)]) for dl in range(2)])
    gradient = jnp.stack([gradient, partner(gradient, "yl")])

    long_raw = lax.all_to_all(long_owned, SEQ, 0, 0, tiled=True).reshape(width, rows)
    wide, tall = (rows, width // 2), (width // 2, rows)

    long_out, gated = run_blocks(
        gate, 2,
        [(long_raw, tall, 0), (query_conv, wide, 1)],
        [((rows, width), F32, wide, 1), ((2, 2, rows, chunk), BF16, (2, 2, rows, LANES), 3)], 2 * 2**20,
    )

    quarter = (1, 2, 2, 2, rows, features)
    (outgoing,) = run_blocks(
        partial_kernel, kinds,
        [place, (gradient, gradient.shape, None), (weight, quarter, 0), (gated, gated.shape, None)],
        [((2, 4, 2, rows, chunk), BF16, (2, 1, 2, rows, chunk), 1)], 6 * 2**20, 2**30,
    )
    arrived = lax.all_to_all(outgoing.reshape(8, 2, rows, chunk), PLANE, 0, 0, tiled=True)
    long_grad, query_conv_grad = run_blocks(
        long_gradient, 2,
        [(arrived, (8, 1, rows, LANES), 3), (query_conv, wide, 1), (long_out, wide, 1)],
        [((width, rows), BF16, tall, 0), ((rows, width), F32, wide, 1)], 3 * 2**20,
    )
    grad_owned = lax.all_to_all(long_grad.reshape(BLOCKS, CHANNELS, LANES), SEQ, 0, 0, tiled=True)

    back_owned, filter_grad = run_kernel(
        backward_kernel,
        [SEQUENCES, jax.ShapeDtypeStruct((CHANNELS, LENGTH), F32)],
        [GRID, TURNED, SECTION], 3,
        grad_owned, filter_spectrum, product_spectrum, steps, turns,
    )

    mixing = arrived.reshape(2, 4, 2, rows, chunk)
    (share,) = run_blocks(
        mix_kernel, kinds,
        [(mixing, ((2, 1, 1, rows, chunk), (0, 1)), 1), (weight, quarter, 0)],
        [((2, 2, 2, rows, features), BF16, (2, 2, 2, rows, features), None)], 6 * 2**20, 2**30,
        [pltpu.VMEM((4, 2 * rows, features), F32)],
    )
    mixed = lax.psum_scatter(
        share.reshape(8 * rows, features), ("xh", "xl", "yl"), scatter_dimension=0, tiled=True
    )

    rim = (2, chunk)
    (query_grad,) = run_blocks(
        query_adjoint, kinds,
        [(query_conv_grad, tokens, 1), (shift(query_conv_grad[:2], -1), rim, 1), (short_taps, taps_block, 2)],
        [((rows, width), BF16, tokens, 1)], 2**20,
    )
    following = shift(jnp.stack([key_conv[:2], value_conv[:2]]), -1)

    back_raw = lax.all_to_all(back_owned, SEQ, 0, 0, tiled=True).reshape(width, rows)
    head, query_grad = lax.optimization_barrier((back_raw[:, :2].T, query_grad))
    after = shift(head, -1)
    key_grad, value_grad = run_blocks(
        key_value_adjoint, kinds,
        [(back_raw, channels, 0), (key_conv, tokens, 1), (value_conv, tokens, 1),
         (after, rim, 1), (following, (2, 2, chunk), 2), (short_taps, taps_block, 2)],
        [((rows, width), BF16, tokens, 1)] * 2, 3 * 2**20,
    )
    return (mixed, query_grad, key_grad, value_grad, filter_grad)


def solution(mesh):
    fine = Mesh(mesh.devices.reshape(tuple(AXES.values())), tuple(AXES))
    token = P(SEQ, TP)
    in_specs = (token, token, token, P(None, None, TP), P(TP + SEQ, None), token, token)
    out_specs = (token, token, token, token, P(TP + SEQ, None))
    return jax.shard_map(
        per_device, mesh=fine, in_specs=in_specs, out_specs=out_specs, check_vma=False
    )
```

```python
import math

import jax
import jax.numpy as jnp
import numpy as np
from jax import lax
from jax.experimental import pallas as pl
from jax.experimental.pallas import tpu as pltpu
from jax.sharding import Mesh
from jax.sharding import PartitionSpec as P

BF16 = jnp.bfloat16
F32 = jnp.float32

AXES = {"xh": 2, "zy": 4, "zh": 2, "zb": 2, "co": 2, "xl": 2, "yh": 2, "yl": 2}
SEQ = ("xh", "zy", "zh", "zb", "co")
TP = ("xl", "yh", "yl")
PLANE = ("xh", "yh", "yl")
COLUMN = ("zy", "zh", "zb", "co")

CHANNELS = 16
BLOCKS = 64
LANES = 128
LENGTH = BLOCKS * LANES

RIM = 16
VMEM_LIMIT = 20 * 2**20
WHOLE_VMEM = 60 * 2**20


def transform_tables():
    blocks = np.arange(BLOCKS)
    lanes = np.arange(LANES)
    first = 2.0 * np.pi * np.outer(blocks + 0.25, blocks) / BLOCKS
    twist = 2.0 * np.pi * np.outer(blocks + 0.25, lanes) / LENGTH
    second = 2.0 * np.pi * (np.outer(lanes, lanes) % LANES) / LANES
    first_table = np.concatenate([np.cos(first), -np.sin(first)], axis=0)
    cosine, sine = np.cos(second), np.sin(second)
    second_table = np.block([[cosine, -sine], [sine, cosine]])
    steps = np.zeros((2 * LANES, 5 * LANES))
    steps[:, : 2 * LANES] = second_table
    steps[:, 2 * LANES : 4 * LANES] = second_table.T
    steps[: 2 * BLOCKS, 4 * LANES : 4 * LANES + BLOCKS] = first_table
    steps[2 * BLOCKS : 3 * BLOCKS, 4 * LANES : 4 * LANES + 2 * BLOCKS] = first_table.T / LENGTH
    turns = np.concatenate([np.cos(twist), np.sin(twist)], axis=1)
    return jnp.asarray(steps, BF16), jnp.asarray(turns, F32)


def to_spectrum(grid_ref, turned_ref, steps, turns):
    first = steps[: 2 * BLOCKS, 4 * LANES : 4 * LANES + BLOCKS]
    cos_twist, sin_twist = turns[:, :LANES], turns[:, LANES:]
    for c in range(CHANNELS):
        grid = grid_ref[pl.ds(c, BLOCKS, stride=CHANNELS), :].astype(BF16)
        section = jnp.dot(first, grid, preferred_element_type=F32)
        real, imag = section[:BLOCKS], section[BLOCKS:]
        rows = slice(c * BLOCKS, (c + 1) * BLOCKS)
        turned_ref[rows, :LANES] = (real * cos_twist + imag * sin_twist).astype(BF16)
        turned_ref[rows, LANES:] = (imag * cos_twist - real * sin_twist).astype(BF16)
    return jnp.dot(turned_ref[...], steps[:, : 2 * LANES], preferred_element_type=F32)


def from_spectrum(spectrum, grid_ref, section_ref, steps, turns):
    first_back = steps[2 * BLOCKS : 3 * BLOCKS, 4 * LANES : 4 * LANES + 2 * BLOCKS]
    cos_twist, sin_twist = turns[:, :LANES], turns[:, LANES:]
    section_ref[...] = jnp.dot(
        spectrum, steps[:, 2 * LANES : 4 * LANES], preferred_element_type=F32
    )
    for c in range(CHANNELS):
        rows = slice(c * BLOCKS, (c + 1) * BLOCKS)
        real, imag = section_ref[rows, :LANES], section_ref[rows, LANES:]
        turned = jnp.concatenate(
            [real * cos_twist - imag * sin_twist, imag * cos_twist + real * sin_twist], axis=0
        ).astype(BF16)
        grid_ref[pl.ds(c, BLOCKS, stride=CHANNELS), :] = jnp.dot(
            first_back, turned, preferred_element_type=F32
        )


def filter_kernel(filter_ref, steps, turns, spectrum_ref, grid, turned):
    for b in range(BLOCKS):
        grid[b * CHANNELS : (b + 1) * CHANNELS, :] = filter_ref[:, b * LANES : (b + 1) * LANES]
    spectrum_ref[...] = to_spectrum(grid, turned, steps, turns).astype(BF16)


def forward_kernel(
    product_ref, filter_spectrum, steps, turns, long_ref, product_spectrum, grid, turned, section
):
    grid[...] = product_ref[...].astype(F32).reshape(BLOCKS * CHANNELS, LANES)
    own = to_spectrum(grid, turned, steps, turns)
    product_spectrum[...] = own.astype(BF16)
    own_re, own_im = own[:, :LANES], own[:, LANES:]
    other = filter_spectrum[...].astype(F32)
    other_re, other_im = other[:, :LANES], other[:, LANES:]
    turned[:, :LANES] = (own_re * other_re - own_im * other_im).astype(BF16)
    turned[:, LANES:] = (own_re * other_im + own_im * other_re).astype(BF16)
    from_spectrum(turned[...], grid, section, steps, turns)
    long_ref[...] = grid[...].reshape(BLOCKS, CHANNELS, LANES).astype(BF16)


def backward_kernel(
    grad_ref, filter_spectrum, product_spectrum, steps, turns,
    back_ref, filter_grad_ref, grid, turned, section,
):
    grid[...] = grad_ref[...].astype(F32).reshape(BLOCKS * CHANNELS, LANES)
    own = to_spectrum(grid, turned, steps, turns)
    own_re, own_im = own[:, :LANES], own[:, LANES:]

    def correlate(other):
        other_re, other_im = other[:, :LANES].astype(F32), other[:, LANES:].astype(F32)
        turned[:, :LANES] = (own_re * other_re + own_im * other_im).astype(BF16)
        turned[:, LANES:] = (own_im * other_re - own_re * other_im).astype(BF16)
        from_spectrum(turned[...], grid, section, steps, turns)

    correlate(filter_spectrum)
    back_ref[...] = grid[...].reshape(BLOCKS, CHANNELS, LANES).astype(BF16)
    correlate(product_spectrum)
    for b in range(BLOCKS):
        filter_grad_ref[:, b * LANES : (b + 1) * LANES] = grid[
            b * CHANNELS : (b + 1) * CHANNELS, :
        ] * (1.0 / math.sqrt(LENGTH))


SPECTRUM = jax.ShapeDtypeStruct((CHANNELS * BLOCKS, 2 * LANES), BF16)
SEQUENCES = jax.ShapeDtypeStruct((BLOCKS, CHANNELS, LANES), BF16)
GRID = pltpu.VMEM((BLOCKS * CHANNELS, LANES), F32)
TURNED = pltpu.VMEM((CHANNELS * BLOCKS, 2 * LANES), BF16)
SECTION = pltpu.VMEM((CHANNELS * BLOCKS, 2 * LANES), F32)


def run_kernel(kernel, out_shape, scratch, transforms, *operands, unread=()):
    in_specs = [
        pl.BlockSpec(memory_space=pl.ANY if i in unread else pltpu.VMEM) for i in range(len(operands))
    ]
    transform_flops = 2 * CHANNELS * BLOCKS * LANES * (2 * BLOCKS + 4 * LANES)
    return pl.pallas_call(
        kernel,
        out_shape=out_shape,
        in_specs=in_specs,
        scratch_shapes=scratch,
        compiler_params=pltpu.CompilerParams(vmem_limit_bytes=VMEM_LIMIT),
        cost_estimate=pl.CostEstimate(
            flops=transforms * transform_flops, bytes_accessed=4 * 2**20, transcendentals=0
        ),
    )(*operands)


def run_blocks(kernel, steps, ins, outs, moved, flops=10**6, scratch=(), limit=VMEM_LIMIT, pinned=False, alias=()):
    def spec(block, axis):
        if block is None:
            return pl.BlockSpec(memory_space=axis or pl.ANY)
        fixed = (0,) * len(block)
        if isinstance(block[0], tuple):
            block, fixed = block
        return pl.BlockSpec(block, lambda i: tuple(i if d == axis else fixed[d] for d in range(len(block))))

    return pl.pallas_call(
        kernel,
        grid=(steps,),
        in_specs=[spec(block, axis) for _, block, axis in ins],
        out_specs=[spec(block, axis) for _, _, block, axis in outs],
        out_shape=[
            (pltpu.HBM if pinned else jax.ShapeDtypeStruct)(shape, dtype) for shape, dtype, _, _ in outs
        ],
        input_output_aliases=dict(alias),
        scratch_shapes=list(scratch),
        compiler_params=pltpu.CompilerParams(vmem_limit_bytes=limit),
        cost_estimate=pl.CostEstimate(flops=flops, bytes_accessed=moved, transcendentals=0),
    )(*[array for array, _, _ in ins])


def row_numbers(value):
    return lax.broadcasted_iota(jnp.int32, value.shape, 0)


def causal(value, before, taps):
    number = row_numbers(value)
    one = jnp.where(number == 0, before[1:2], pltpu.roll(value, 1, 0))
    two = jnp.where(number == 0, before[0:1], pltpu.roll(value, 2, 0))
    two = jnp.where(number == 1, before[1:2], two)
    return taps[0:1] * value + taps[1:2] * one + taps[2:3] * two


def adjoint(value, after, taps):
    rows = value.shape[0]
    number = row_numbers(value)
    one = jnp.where(number == rows - 1, after[0:1], pltpu.roll(value, rows - 1, 0))
    two = jnp.where(number == rows - 1, after[1:2], pltpu.roll(value, rows - 2, 0))
    two = jnp.where(number == rows - 2, after[0:1], two)
    return taps[0:1] * value + taps[1:2] * one + taps[2:3] * two


def filter_product(k_ref, v_ref, before_ref, taps_ref, product_ref):
    kc = causal(k_ref[...].astype(F32), before_ref[1].astype(F32), taps_ref[1])
    vc = causal(v_ref[...].astype(F32), before_ref[2].astype(F32), taps_ref[2])
    product_ref[...] = (kc * vc).T.astype(BF16)


def filter_inputs(
    q_ref, k_ref, v_ref, before_ref, taps_ref, _, qc_ref, kc_ref, vc_ref, turned_ref
):
    sources, results = (q_ref, k_ref, v_ref), (qc_ref, kc_ref, vc_ref)
    for i in range(3):
        results[i][...] = causal(sources[i][...].astype(F32), before_ref[i].astype(F32), taps_ref[i])
    turned_ref[...] = qc_ref[...].T


def gate(long_ref, qc_ref, gated_ref):
    gated = (qc_ref[...] * long_ref[...].astype(F32).T).astype(BF16)
    for co in range(2):
        for y in range(4):
            start = (2 * (y % 2) + co) * LANES
            gated_ref[co, y] = gated[:, start : start + LANES]


def partial_kernel(place_ref, gradient_ref, weight_ref, _, out_ref, total):
    xh, xl, yl = place_ref[0], place_ref[1], place_ref[3]
    step = pl.program_id(0)
    features, tokens = gradient_ref.shape[2:]
    rows = tokens // 2
    added = jnp.dot(
        weight_ref[...].reshape(total.shape[0], features),
        gradient_ref[(step // 2) ^ yl, (step % 2) ^ xl],
        preferred_element_type=F32,
    )

    @pl.when(step == 0)
    def _():
        total[...] = added

    @pl.when(step > 0)
    def _():
        total[...] += added

    @pl.when(step == pl.num_programs(0) - 1)
    def _():
        for t in range(2):
            value = total[:, t * rows : (t + 1) * rows].astype(BF16)
            out_ref[t ^ xh] = value.reshape(out_ref.shape[1:])


def long_gradient(parts_ref, qc_ref, long_ref, grad_ref, qg_ref):
    for e in range(2):
        for r in range(2):
            rows = slice((2 * e + r) * LANES, (2 * e + r + 1) * LANES)
            gated_grad = parts_ref[4 * r + e].astype(F32) + parts_ref[4 * r + 2 + e].astype(F32)
            grad_ref[rows] = (qc_ref[rows] * gated_grad).astype(BF16)
            qg_ref[rows] = gated_grad * long_ref[rows].astype(F32)


def mix_kernel(gated_ref, weight_ref, out_ref, total):
    halves, _, rows, width = gated_ref.shape
    features = weight_ref.shape[4]
    step = pl.program_id(0)

    @pl.when(step == 0)
    def _():
        total[...] = jnp.zeros_like(total)

    gated = gated_ref[...].reshape(halves * rows, width)
    for e in range(2):
        for f in range(2):
            total[2 * e + f] += jnp.dot(
                gated, weight_ref[0, :, 2 * e + f].reshape(width, features), preferred_element_type=F32
            )

    @pl.when(step == pl.num_programs(0) - 1)
    def _():
        for e in range(2):
            for f in range(2):
                for t in range(2):
                    out_ref[t, f, e] = total[2 * e + f, t * rows : (t + 1) * rows].astype(BF16)


def query_adjoint(qg_ref, after_ref, taps_ref, out_ref):
    out_ref[...] = adjoint(qg_ref[...].T, after_ref[...], taps_ref[0]).astype(BF16)


def key_value_adjoint(back_ref, kc_ref, vc_ref, taps_ref, key_ref, value_ref):
    back = back_ref[...].astype(F32).T
    after = jnp.zeros((2, back.shape[1]), F32)
    key_ref[...] = adjoint(back * vc_ref[...], after, taps_ref[1]).astype(BF16)
    value_ref[...] = adjoint(back * kc_ref[...], after, taps_ref[2]).astype(BF16)


def key_value_rim(
    tail_ref, kc_ref, vc_ref, after_ref, next_ref, taps_ref, _, __, key_ref, value_ref
):
    back = tail_ref[...].astype(F32)
    after = after_ref[...].astype(F32)
    key_ref[...] = adjoint(back * vc_ref[...], after * next_ref[1], taps_ref[1]).astype(BF16)
    value_ref[...] = adjoint(back * kc_ref[...], after * next_ref[0], taps_ref[2]).astype(BF16)


def shift(value, steps):
    count = 1
    for axis in SEQ:
        count *= lax.axis_size(axis)
    first, last = max(0, -steps), min(count, count - steps)
    return lax.ppermute(value, SEQ, [(i, i + steps) for i in range(first, last)])


def partner(value, axis):
    return lax.ppermute(value, axis, [(0, 1), (1, 0)])


def across(value, dx, dl):
    if not (dx or dl):
        return value
    return lax.ppermute(value, ("xh", "xl"), [(i, i ^ (2 * dx + dl)) for i in range(4)])


def turn(value):
    pairs = []
    for i in range(32):
        a, s, c, b, e = ((i >> k) & 1 for k in (4, 3, 2, 1, 0))
        pairs.append((i, 16 * c + 8 * e + 4 * b + 2 * a + s))
    return lax.ppermute(value, ("xh", "zb", "co", "xl", "yl"), pairs)


def per_device(queries, keys, values, short_taps, long_filter, out_weight, cotangent):
    rows, width = queries.shape
    features = out_weight.shape[1]
    place = jnp.stack([lax.axis_index(axis) for axis in ("xh", "xl", "yh", "yl")])
    place = (place.astype(jnp.int32), None, pltpu.SMEM)
    kinds, chunk = 4, width // 4

    rims = jnp.stack([x[rows - 2 :] for x in (queries, keys, values)])
    rims, out_weight = lax.optimization_barrier((rims, out_weight))
    before, turned = lax.optimization_barrier((shift(rims, 1), turn(out_weight)))
    weight = lax.all_gather(turned, COLUMN, axis=0).reshape(4, 2, 4, rows, features)
    weight = pltpu.with_memory_space_constraint(weight, pltpu.HBM)

    steps, turns = transform_tables()
    filter_spectrum = run_kernel(filter_kernel, SPECTRUM, [GRID, TURNED], 1, long_filter, steps, turns)

    tokens = (rows, chunk)
    channels = (chunk, rows)
    taps_block = (3, 3, chunk)
    plane = ((rows, width), F32, tokens, 1)
    (product,) = run_blocks(
        filter_product, 1,
        [(keys, (rows, width), 1), (values, (rows, width), 1), (before, before.shape, 2), (short_taps, short_taps.shape, 2)],
        [((width, rows), BF16, (width, rows), 0)], 2**20, limit=WHOLE_VMEM,
    )
    query_conv, key_conv, value_conv, query_turned = run_blocks(
        filter_inputs, kinds,
        [(queries, tokens, 1), (keys, tokens, 1), (values, tokens, 1),
         (before, (3, 2, chunk), 2), (short_taps, taps_block, 2), (product, None, None)],
        [plane, plane, plane, ((width, rows), F32, channels, 0)], 3 * 2**20, limit=WHOLE_VMEM,
    )

    product_owned = lax.all_to_all(product.reshape(BLOCKS, CHANNELS, LANES), SEQ, 0, 0, tiled=True)
    long_owned, product_spectrum = run_kernel(
        forward_kernel, [pltpu.HBM(SEQUENCES.shape, BF16), pltpu.HBM(SPECTRUM.shape, BF16)], [GRID, TURNED, SECTION], 2,
        product_owned, filter_spectrum, steps, turns,
    )
    turned = cotangent.T
    gradient = jnp.stack(
        [jnp.concatenate([across(turned, dx, dl) for dx in range(2)], axis=1) for dl in range(2)]
    )
    gradient = jnp.stack([gradient, partner(gradient, "yl")])

    long_raw = lax.all_to_all(long_owned, SEQ, 0, 0, tiled=True).reshape(width, rows)
    wide, tall = (rows, width // 2), (width // 2, rows)

    (gated,) = run_blocks(
        gate, 2,
        [(long_raw, tall, 0), (query_conv, wide, 1)],
        [((2, 4, rows, chunk), BF16, (2, 4, rows, LANES), 3)], 2 * 2**20, pinned=True,
    )

    mixing = lax.all_to_all(gated.reshape(8, rows, chunk), PLANE, 0, 0, tiled=True)

    (partial,) = run_blocks(
        partial_kernel, kinds,
        [place, (gradient, gradient.shape, None),
         (weight, (4, 2, 1, rows, features), 2), (mixing, None, None)],
        [((2, 4, chunk, rows), BF16, (2, 4, chunk, rows), None)], 6 * 2**20, 2**30,
        [pltpu.VMEM((width, 2 * rows), F32)],
    )
    arrived = lax.all_to_all(partial.reshape(8, chunk, rows), PLANE, 0, 0, tiled=True)
    long_grad, query_conv_grad = run_blocks(
        long_gradient, 2,
        [(arrived, (8, LANES, rows), 1), (query_turned, tall, 0), (long_raw, tall, 0)],
        [((width, rows), BF16, tall, 0), ((width, rows), F32, tall, 0)], 3 * 2**20, pinned=True,
    )
    grad_owned = lax.all_to_all(long_grad.reshape(BLOCKS, CHANNELS, LANES), SEQ, 0, 0, tiled=True)

    back_owned, filter_grad = run_kernel(
        backward_kernel,
        [pltpu.HBM(SEQUENCES.shape, BF16), pltpu.HBM((CHANNELS, LENGTH), F32)],
        [GRID, TURNED, SECTION], 3,
        grad_owned, filter_spectrum, product_spectrum, steps, turns,
    )

    quarter = (1, 2, 4, rows, features)
    (share,) = run_blocks(
        mix_kernel, kinds,
        [(mixing.reshape(2, 4, rows, chunk), (2, 1, rows, chunk), 1), (weight, quarter, 0)],
        [((2, 2, 2, rows, features), BF16, (2, 2, 2, rows, features), None)], 6 * 2**20, 2**30,
        [pltpu.VMEM((4, 2 * rows, features), F32)],
    )
    mixed = lax.psum_scatter(
        share.reshape(8 * rows, features), ("xh", "xl", "yl"), scatter_dimension=0, tiled=True
    )

    rim = (2, chunk)
    (query_grad,) = run_blocks(
        query_adjoint, kinds,
        [(query_conv_grad, channels, 0), (shift(query_conv_grad[:, :2].T, -1), rim, 1), (short_taps, taps_block, 2)],
        [((rows, width), BF16, tokens, 1)], 2**20,
    )
    following = shift(jnp.stack([key_conv[:2], value_conv[:2]]), -1)

    back_raw = lax.all_to_all(back_owned, SEQ, 0, 0, tiled=True).reshape(width, rows)
    head, query_grad = lax.optimization_barrier((back_raw[:, :2].T, query_grad))
    after = shift(head, -1)
    grads = run_blocks(
        key_value_adjoint, kinds,
        [(back_raw, channels, 0), (key_conv, tokens, 1), (value_conv, tokens, 1), (short_taps, taps_block, 2)],
        [((rows, width), BF16, tokens, 1)] * 2, 3 * 2**20,
    )
    tail = (RIM, width)
    last = (tail, (rows // RIM - 1, 0))
    key_grad, value_grad = run_blocks(
        key_value_rim, 1,
        [(back_raw[:, rows - RIM :].T, tail, None), (key_conv, last, None), (value_conv, last, None),
         (after, (2, width), None), (following, (2, 2, width), None), (short_taps, (3, 3, width), None),
         (grads[0], None, None), (grads[1], None, None)],
        [((rows, width), BF16, last, None)] * 2, 2**20, alias=((6, 0), (7, 1)),
    )
    return (mixed, query_grad, key_grad, value_grad, filter_grad)


def solution(mesh):
    fine = Mesh(mesh.devices.reshape(tuple(AXES.values())), tuple(AXES))
    token = P(SEQ, TP)
    in_specs = (token, token, token, P(None, None, TP), P(TP + SEQ, None), token, token)
    out_specs = (token, token, token, token, P(TP + SEQ, None))
    return jax.shard_map(
        per_device, mesh=fine, in_specs=in_specs, out_specs=out_specs, check_vma=False
    )
```

```python
import math

import jax
import jax.numpy as jnp
import numpy as np
from jax import lax
from jax.experimental import pallas as pl
from jax.experimental.pallas import tpu as pltpu
from jax.sharding import Mesh
from jax.sharding import PartitionSpec as P

BF16 = jnp.bfloat16
F32 = jnp.float32

AXES = {"xh": 2, "zy": 4, "zh": 2, "zb": 2, "co": 2, "xl": 2, "yh": 2, "yl": 2}
SEQ = ("xh", "zy", "zh", "zb", "co")
TP = ("xl", "yh", "yl")
PLANE = ("xh", "yh", "yl")
COLUMN = ("zy", "zh", "zb", "co")

CHANNELS = 16
BLOCKS = 64
LANES = 128
LENGTH = BLOCKS * LANES

RIM = 16
VMEM_LIMIT = 20 * 2**20
WHOLE_VMEM = 60 * 2**20


def transform_tables():
    blocks = np.arange(BLOCKS)
    lanes = np.arange(LANES)
    first = 2.0 * np.pi * np.outer(blocks + 0.25, blocks) / BLOCKS
    twist = 2.0 * np.pi * np.outer(blocks + 0.25, lanes) / LENGTH
    second = 2.0 * np.pi * (np.outer(lanes, lanes) % LANES) / LANES
    first_table = np.concatenate([np.cos(first), -np.sin(first)], axis=0)
    cosine, sine = np.cos(second), np.sin(second)
    second_table = np.block([[cosine, -sine], [sine, cosine]])
    steps = np.zeros((2 * LANES + BLOCKS, 5 * LANES))
    steps[: 2 * LANES, : 2 * LANES] = second_table
    steps[: 2 * LANES, 2 * LANES : 4 * LANES] = second_table.T
    steps[: 2 * BLOCKS, 4 * LANES : 4 * LANES + BLOCKS] = first_table
    steps[2 * BLOCKS : 3 * BLOCKS, 4 * LANES : 4 * LANES + 2 * BLOCKS] = first_table.T / LENGTH
    turns = np.concatenate([np.cos(twist), np.sin(twist)], axis=1)
    coarse = turns.astype(BF16).astype(np.float64)
    steps[2 * LANES :, : 2 * LANES] = coarse
    steps[2 * LANES :, 2 * LANES : 4 * LANES] = turns - coarse
    return jnp.asarray(steps, BF16)


def twist_of(steps):
    parts = steps[2 * LANES :].astype(F32)
    turns = parts[:, : 2 * LANES] + parts[:, 2 * LANES : 4 * LANES]
    return turns[:, :LANES], turns[:, LANES:]


def to_spectrum(grid_ref, turned_ref, steps):
    first = steps[: 2 * BLOCKS, 4 * LANES : 4 * LANES + BLOCKS]
    cos_twist, sin_twist = twist_of(steps)
    for c in range(CHANNELS):
        grid = grid_ref[pl.ds(c, BLOCKS, stride=CHANNELS), :].astype(BF16)
        section = jnp.dot(first, grid, preferred_element_type=F32)
        real, imag = section[:BLOCKS], section[BLOCKS:]
        rows = slice(c * BLOCKS, (c + 1) * BLOCKS)
        turned_ref[rows, :LANES] = (real * cos_twist + imag * sin_twist).astype(BF16)
        turned_ref[rows, LANES:] = (imag * cos_twist - real * sin_twist).astype(BF16)
    return jnp.dot(turned_ref[...], steps[: 2 * LANES, : 2 * LANES], preferred_element_type=F32)


def from_spectrum(spectrum, grid_ref, section_ref, steps):
    first_back = steps[2 * BLOCKS : 3 * BLOCKS, 4 * LANES : 4 * LANES + 2 * BLOCKS]
    cos_twist, sin_twist = twist_of(steps)
    section_ref[...] = jnp.dot(
        spectrum, steps[: 2 * LANES, 2 * LANES : 4 * LANES], preferred_element_type=F32
    )
    for c in range(CHANNELS):
        rows = slice(c * BLOCKS, (c + 1) * BLOCKS)
        real, imag = section_ref[rows, :LANES], section_ref[rows, LANES:]
        turned = jnp.concatenate(
            [real * cos_twist - imag * sin_twist, imag * cos_twist + real * sin_twist], axis=0
        ).astype(BF16)
        grid_ref[pl.ds(c, BLOCKS, stride=CHANNELS), :] = jnp.dot(
            first_back, turned, preferred_element_type=F32
        )


def filter_kernel(filter_ref, steps, spectrum_ref, grid, turned):
    for b in range(BLOCKS):
        grid[b * CHANNELS : (b + 1) * CHANNELS, :] = filter_ref[:, b * LANES : (b + 1) * LANES]
    spectrum_ref[...] = to_spectrum(grid, turned, steps).astype(BF16)


def forward_kernel(
    product_ref, filter_spectrum, steps, long_ref, product_spectrum, grid, turned, section
):
    grid[...] = product_ref[...].astype(F32).reshape(BLOCKS * CHANNELS, LANES)
    own = to_spectrum(grid, turned, steps)
    product_spectrum[...] = own.astype(BF16)
    own_re, own_im = own[:, :LANES], own[:, LANES:]
    other = filter_spectrum[...].astype(F32)
    other_re, other_im = other[:, :LANES], other[:, LANES:]
    turned[:, :LANES] = (own_re * other_re - own_im * other_im).astype(BF16)
    turned[:, LANES:] = (own_re * other_im + own_im * other_re).astype(BF16)
    from_spectrum(turned[...], grid, section, steps)
    long_ref[...] = grid[...].reshape(BLOCKS, CHANNELS, LANES).astype(BF16)


def correlate(grad_ref, other, grid, turned, section, steps):
    grid[...] = grad_ref[...].astype(F32).reshape(BLOCKS * CHANNELS, LANES)
    own = to_spectrum(grid, turned, steps)
    own_re, own_im = own[:, :LANES], own[:, LANES:]
    other_re, other_im = other[:, :LANES].astype(F32), other[:, LANES:].astype(F32)
    turned[:, :LANES] = (own_re * other_re + own_im * other_im).astype(BF16)
    turned[:, LANES:] = (own_im * other_re - own_re * other_im).astype(BF16)
    from_spectrum(turned[...], grid, section, steps)


def backward_kernel(grad_ref, filter_spectrum, steps, back_ref, grid, turned, section):
    correlate(grad_ref, filter_spectrum, grid, turned, section, steps)
    back_ref[...] = grid[...].reshape(BLOCKS, CHANNELS, LANES).astype(BF16)


def filter_grad_kernel(
    grad_ref, product_spectrum, steps, _, filter_grad_ref, grid, turned, section
):
    correlate(grad_ref, product_spectrum, grid, turned, section, steps)
    for b in range(BLOCKS):
        filter_grad_ref[:, b * LANES : (b + 1) * LANES] = grid[
            b * CHANNELS : (b + 1) * CHANNELS, :
        ] * (1.0 / math.sqrt(LENGTH))


SPECTRUM = jax.ShapeDtypeStruct((CHANNELS * BLOCKS, 2 * LANES), BF16)
SEQUENCES = jax.ShapeDtypeStruct((BLOCKS, CHANNELS, LANES), BF16)
GRID = pltpu.VMEM((BLOCKS * CHANNELS, LANES), F32)
TURNED = pltpu.VMEM((CHANNELS * BLOCKS, 2 * LANES), BF16)
SECTION = pltpu.VMEM((CHANNELS * BLOCKS, 2 * LANES), F32)


def run_kernel(kernel, out_shape, scratch, transforms, *operands, unread=()):
    in_specs = [
        pl.BlockSpec(memory_space=pl.ANY if i in unread else pltpu.VMEM) for i in range(len(operands))
    ]
    transform_flops = 2 * CHANNELS * BLOCKS * LANES * (2 * BLOCKS + 4 * LANES)
    return pl.pallas_call(
        kernel,
        out_shape=out_shape,
        in_specs=in_specs,
        scratch_shapes=scratch,
        compiler_params=pltpu.CompilerParams(vmem_limit_bytes=VMEM_LIMIT),
        cost_estimate=pl.CostEstimate(
            flops=transforms * transform_flops, bytes_accessed=4 * 2**20, transcendentals=0
        ),
    )(*operands)


def run_blocks(kernel, steps, ins, outs, moved, flops=10**6, scratch=(), limit=VMEM_LIMIT, pinned=False, alias=()):
    def spec(block, axis):
        if block is None:
            return pl.BlockSpec(memory_space=axis or pl.ANY)
        fixed = (0,) * len(block)
        if isinstance(block[0], tuple):
            block, fixed = block
        return pl.BlockSpec(block, lambda i: tuple(i if d == axis else fixed[d] for d in range(len(block))))

    return pl.pallas_call(
        kernel,
        grid=(steps,),
        in_specs=[spec(block, axis) for _, block, axis in ins],
        out_specs=[spec(block, axis) for _, _, block, axis in outs],
        out_shape=[
            (pltpu.HBM if pinned else jax.ShapeDtypeStruct)(shape, dtype) for shape, dtype, _, _ in outs
        ],
        input_output_aliases=dict(alias),
        scratch_shapes=list(scratch),
        compiler_params=pltpu.CompilerParams(vmem_limit_bytes=limit),
        cost_estimate=pl.CostEstimate(flops=flops, bytes_accessed=moved, transcendentals=0),
    )(*[array for array, _, _ in ins])


def row_numbers(value):
    return lax.broadcasted_iota(jnp.int32, value.shape, 0)


def causal(value, before, taps):
    number = row_numbers(value)
    one = jnp.where(number == 0, before[1:2], pltpu.roll(value, 1, 0))
    two = jnp.where(number == 0, before[0:1], pltpu.roll(value, 2, 0))
    two = jnp.where(number == 1, before[1:2], two)
    return taps[0:1] * value + taps[1:2] * one + taps[2:3] * two


def adjoint(value, after, taps):
    rows = value.shape[0]
    number = row_numbers(value)
    one = jnp.where(number == rows - 1, after[0:1], pltpu.roll(value, rows - 1, 0))
    two = jnp.where(number == rows - 1, after[1:2], pltpu.roll(value, rows - 2, 0))
    two = jnp.where(number == rows - 2, after[0:1], two)
    return taps[0:1] * value + taps[1:2] * one + taps[2:3] * two


def filter_product(k_ref, v_ref, before_ref, taps_ref, product_ref):
    kc = causal(k_ref[...].astype(F32), before_ref[1].astype(F32), taps_ref[1])
    vc = causal(v_ref[...].astype(F32), before_ref[2].astype(F32), taps_ref[2])
    product_ref[...] = (kc * vc).T.astype(BF16)


def filter_inputs(
    q_ref, k_ref, v_ref, before_ref, taps_ref, _, qc_ref, kc_ref, vc_ref, turned_ref
):
    sources, results = (q_ref, k_ref, v_ref), (qc_ref, kc_ref, vc_ref)
    for i in range(3):
        results[i][...] = causal(sources[i][...].astype(F32), before_ref[i].astype(F32), taps_ref[i])
    turned_ref[...] = qc_ref[...].T


def gate(long_ref, qc_ref, gated_ref):
    gated = (qc_ref[...] * long_ref[...].astype(F32).T).astype(BF16)
    for co in range(2):
        for y in range(4):
            start = (2 * (y % 2) + co) * LANES
            gated_ref[co, y] = gated[:, start : start + LANES]


def partial_kernel(place_ref, gradient_ref, weight_ref, _, out_ref, total):
    xh, xl, yl = place_ref[0], place_ref[1], place_ref[3]
    step = pl.program_id(0)
    features, tokens = gradient_ref.shape[2:]
    rows = tokens // 2
    added = jnp.dot(
        weight_ref[...].reshape(total.shape[0], features),
        gradient_ref[(step // 2) ^ yl, (step % 2) ^ xl],
        preferred_element_type=F32,
    )

    @pl.when(step == 0)
    def _():
        total[...] = added

    @pl.when(step > 0)
    def _():
        total[...] += added

    @pl.when(step == pl.num_programs(0) - 1)
    def _():
        for t in range(2):
            value = total[:, t * rows : (t + 1) * rows].astype(BF16)
            out_ref[t ^ xh] = value.reshape(out_ref.shape[1:])


def long_gradient(parts_ref, qc_ref, long_ref, grad_ref, qg_ref):
    for e in range(2):
        for r in range(2):
            rows = slice((2 * e + r) * LANES, (2 * e + r + 1) * LANES)
            gated_grad = parts_ref[4 * r + e].astype(F32) + parts_ref[4 * r + 2 + e].astype(F32)
            grad_ref[rows] = (qc_ref[rows] * gated_grad).astype(BF16)
            qg_ref[rows] = gated_grad * long_ref[rows].astype(F32)


def mix_kernel(gated_ref, weight_ref, out_ref, total):
    halves, _, rows, width = gated_ref.shape
    features = weight_ref.shape[4]
    step = pl.program_id(0)

    @pl.when(step == 0)
    def _():
        total[...] = jnp.zeros_like(total)

    gated = gated_ref[...].reshape(halves * rows, width)
    for e in range(2):
        for f in range(2):
            total[2 * e + f] += jnp.dot(
                gated, weight_ref[0, :, 2 * e + f].reshape(width, features), preferred_element_type=F32
            )

    @pl.when(step == pl.num_programs(0) - 1)
    def _():
        for e in range(2):
            for f in range(2):
                for t in range(2):
                    out_ref[t, f, e] = total[2 * e + f, t * rows : (t + 1) * rows].astype(BF16)


def query_adjoint(qg_ref, after_ref, taps_ref, out_ref):
    out_ref[...] = adjoint(qg_ref[...].T, after_ref[...], taps_ref[0]).astype(BF16)


def key_value_adjoint(back_ref, kc_ref, vc_ref, taps_ref, key_ref, value_ref):
    back = back_ref[...].astype(F32).T
    after = jnp.zeros((2, back.shape[1]), F32)
    key_ref[...] = adjoint(back * vc_ref[...], after, taps_ref[1]).astype(BF16)
    value_ref[...] = adjoint(back * kc_ref[...], after, taps_ref[2]).astype(BF16)


def key_value_rim(
    tail_ref, kc_ref, vc_ref, after_ref, next_ref, taps_ref, _, __, key_ref, value_ref
):
    back = tail_ref[...].astype(F32)
    after = after_ref[...].astype(F32)
    key_ref[...] = adjoint(back * vc_ref[...], after * next_ref[1], taps_ref[1]).astype(BF16)
    value_ref[...] = adjoint(back * kc_ref[...], after * next_ref[0], taps_ref[2]).astype(BF16)


def shift(value, steps):
    count = 1
    for axis in SEQ:
        count *= lax.axis_size(axis)
    first, last = max(0, -steps), min(count, count - steps)
    return lax.ppermute(value, SEQ, [(i, i + steps) for i in range(first, last)])


def partner(value, axis):
    return lax.ppermute(value, axis, [(0, 1), (1, 0)])


def across(value, dx, dl):
    if not (dx or dl):
        return value
    return lax.ppermute(value, ("xh", "xl"), [(i, i ^ (2 * dx + dl)) for i in range(4)])


def turn(value):
    pairs = []
    for i in range(32):
        a, s, c, b, e = ((i >> k) & 1 for k in (4, 3, 2, 1, 0))
        pairs.append((i, 16 * c + 8 * e + 4 * b + 2 * a + s))
    return lax.ppermute(value, ("xh", "zb", "co", "xl", "yl"), pairs)


def per_device(queries, keys, values, short_taps, long_filter, out_weight, cotangent):
    rows, width = queries.shape
    features = out_weight.shape[1]
    place = jnp.stack([lax.axis_index(axis) for axis in ("xh", "xl", "yh", "yl")])
    place = (place.astype(jnp.int32), None, pltpu.SMEM)
    kinds, chunk = 4, width // 4

    rims = jnp.stack([x[rows - 2 :] for x in (queries, keys, values)])
    rims, out_weight = lax.optimization_barrier((rims, out_weight))
    before, turned = lax.optimization_barrier((shift(rims, 1), turn(out_weight)))
    weight = lax.all_gather(turned, COLUMN, axis=0).reshape(4, 2, 4, rows, features)
    weight = pltpu.with_memory_space_constraint(weight, pltpu.HBM)

    steps = transform_tables()
    filter_spectrum = run_kernel(filter_kernel, SPECTRUM, [GRID, TURNED], 1, long_filter, steps)

    tokens = (rows, chunk)
    channels = (chunk, rows)
    taps_block = (3, 3, chunk)
    plane = ((rows, width), F32, tokens, 1)
    (product,) = run_blocks(
        filter_product, 1,
        [(keys, (rows, width), 1), (values, (rows, width), 1), (before, before.shape, 2), (short_taps, short_taps.shape, 2)],
        [((width, rows), BF16, (width, rows), 0)], 2**20, limit=WHOLE_VMEM,
    )
    query_conv, key_conv, value_conv, query_turned = run_blocks(
        filter_inputs, kinds,
        [(queries, tokens, 1), (keys, tokens, 1), (values, tokens, 1),
         (before, (3, 2, chunk), 2), (short_taps, taps_block, 2), (product, None, None)],
        [plane, plane, plane, ((width, rows), F32, channels, 0)], 3 * 2**20, limit=WHOLE_VMEM,
    )

    product_owned = lax.all_to_all(product.reshape(BLOCKS, CHANNELS, LANES), SEQ, 0, 0, tiled=True)
    long_owned, product_spectrum = run_kernel(
        forward_kernel, [pltpu.HBM(SEQUENCES.shape, BF16), pltpu.HBM(SPECTRUM.shape, BF16)], [GRID, TURNED, SECTION], 2,
        product_owned, filter_spectrum, steps,
    )
    turned = cotangent.T
    gradient = jnp.stack(
        [jnp.concatenate([across(turned, dx, dl) for dx in range(2)], axis=1) for dl in range(2)]
    )
    gradient = jnp.stack([gradient, partner(gradient, "yl")])

    long_raw = lax.all_to_all(long_owned, SEQ, 0, 0, tiled=True).reshape(width, rows)
    wide, tall = (rows, width // 2), (width // 2, rows)

    (gated,) = run_blocks(
        gate, 2,
        [(long_raw, tall, 0), (query_conv, wide, 1)],
        [((2, 4, rows, chunk), BF16, (2, 4, rows, LANES), 3)], 2 * 2**20, pinned=True,
    )

    mixing = lax.all_to_all(gated.reshape(8, rows, chunk), PLANE, 0, 0, tiled=True)

    (partial,) = run_blocks(
        partial_kernel, kinds,
        [place, (gradient, gradient.shape, None),
         (weight, (4, 2, 1, rows, features), 2), (mixing, None, None)],
        [((2, 4, chunk, rows), BF16, (2, 4, chunk, rows), None)], 6 * 2**20, 2**30,
        [pltpu.VMEM((width, 2 * rows), F32)],
    )
    arrived = lax.all_to_all(partial.reshape(8, chunk, rows), PLANE, 0, 0, tiled=True)
    long_grad, query_conv_grad = run_blocks(
        long_gradient, 2,
        [(arrived, (8, LANES, rows), 1), (query_turned, tall, 0), (long_raw, tall, 0)],
        [((width, rows), BF16, tall, 0), ((width, rows), F32, tall, 0)], 3 * 2**20, pinned=True,
    )
    grad_owned = lax.all_to_all(long_grad.reshape(BLOCKS, CHANNELS, LANES), SEQ, 0, 0, tiled=True)

    back_owned = run_kernel(
        backward_kernel, pltpu.HBM(SEQUENCES.shape, BF16), [GRID, TURNED, SECTION], 2,
        grad_owned, filter_spectrum, steps,
    )
    filter_grad = run_kernel(
        filter_grad_kernel, jax.ShapeDtypeStruct((CHANNELS, LENGTH), F32), [GRID, TURNED, SECTION], 2,
        grad_owned, product_spectrum, steps, back_owned, unread=(3,),
    )

    quarter = (1, 2, 4, rows, features)
    (share,) = run_blocks(
        mix_kernel, kinds,
        [(mixing.reshape(2, 4, rows, chunk), (2, 1, rows, chunk), 1), (weight, quarter, 0)],
        [((2, 2, 2, rows, features), BF16, (2, 2, 2, rows, features), None)], 6 * 2**20, 2**30,
        [pltpu.VMEM((4, 2 * rows, features), F32)],
    )
    mixed = lax.psum_scatter(
        share.reshape(8 * rows, features), ("xh", "xl", "yl"), scatter_dimension=0, tiled=True
    )

    rim = (2, chunk)
    (query_grad,) = run_blocks(
        query_adjoint, kinds,
        [(query_conv_grad, channels, 0), (shift(query_conv_grad[:, :2].T, -1), rim, 1), (short_taps, taps_block, 2)],
        [((rows, width), BF16, tokens, 1)], 2**20,
    )
    following = shift(jnp.stack([key_conv[:2], value_conv[:2]]), -1)

    back_raw = lax.all_to_all(back_owned, SEQ, 0, 0, tiled=True).reshape(width, rows)
    head, query_grad, filter_grad = lax.optimization_barrier((back_raw[:, :2].T, query_grad, filter_grad))
    after = shift(head, -1)
    grads = run_blocks(
        key_value_adjoint, kinds,
        [(back_raw, channels, 0), (key_conv, tokens, 1), (value_conv, tokens, 1), (short_taps, taps_block, 2)],
        [((rows, width), BF16, tokens, 1)] * 2, 3 * 2**20,
    )
    tail = (RIM, width)
    last = (tail, (rows // RIM - 1, 0))
    key_grad, value_grad = run_blocks(
        key_value_rim, 1,
        [(back_raw[:, rows - RIM :].T, tail, None), (key_conv, last, None), (value_conv, last, None),
         (after, (2, width), None), (following, (2, 2, width), None), (short_taps, (3, 3, width), None),
         (grads[0], None, None), (grads[1], None, None)],
        [((rows, width), BF16, last, None)] * 2, 2**20, alias=((6, 0), (7, 1)),
    )
    return (mixed, query_grad, key_grad, value_grad, filter_grad)


def solution(mesh):
    fine = Mesh(mesh.devices.reshape(tuple(AXES.values())), tuple(AXES))
    token = P(SEQ, TP)
    in_specs = (token, token, token, P(None, None, TP), P(TP + SEQ, None), token, token)
    out_specs = (token, token, token, token, P(TP + SEQ, None))
    return jax.shard_map(
        per_device, mesh=fine, in_specs=in_specs, out_specs=out_specs, check_vma=False
    )
```

```python
import math

import jax
import jax.numpy as jnp
import numpy as np
from jax import lax
from jax.experimental import pallas as pl
from jax.experimental.pallas import tpu as pltpu
from jax.sharding import Mesh
from jax.sharding import PartitionSpec as P

BF16 = jnp.bfloat16
F32 = jnp.float32

AXES = {"xh": 2, "zy": 4, "zh": 2, "zb": 2, "co": 2, "xl": 2, "yh": 2, "yl": 2}
SEQ = ("xh", "zy", "zh", "zb", "co")
TP = ("xl", "yh", "yl")
PLANE = ("xh", "yh", "yl")
COLUMN = ("zy", "zh", "zb", "co")

CHANNELS = 16
BLOCKS = 64
LANES = 128
LENGTH = BLOCKS * LANES
ROWS = BLOCKS * CHANNELS

RIM = 16
VMEM_LIMIT = 20 * 2**20
WHOLE_VMEM = 60 * 2**20


def transform_tables():
    blocks = np.arange(BLOCKS)
    lanes = np.arange(LANES)
    first = 2.0 * np.pi * np.outer(blocks + 0.25, blocks) / BLOCKS
    twist = 2.0 * np.pi * np.outer(blocks + 0.25, lanes) / LENGTH
    second = 2.0 * np.pi * (np.outer(lanes, lanes) % LANES) / LANES
    first_table = np.concatenate([np.cos(first), -np.sin(first)], axis=0)
    cosine, sine = np.cos(second), np.sin(second)
    second_table = np.block([[cosine, -sine], [sine, cosine]])
    steps = np.zeros((2 * LANES + BLOCKS, 5 * LANES))
    steps[: 2 * LANES, : 2 * LANES] = second_table
    steps[: 2 * LANES, 2 * LANES : 4 * LANES] = second_table.T
    steps[: 2 * BLOCKS, 4 * LANES : 4 * LANES + BLOCKS] = first_table
    steps[2 * BLOCKS : 3 * BLOCKS, 4 * LANES : 4 * LANES + 2 * BLOCKS] = first_table.T / LENGTH
    turns = np.concatenate([np.cos(twist), np.sin(twist)], axis=1)
    coarse = turns.astype(BF16).astype(np.float64)
    steps[2 * LANES :, : 2 * LANES] = coarse
    steps[2 * LANES :, 2 * LANES : 4 * LANES] = turns - coarse
    return jnp.asarray(steps, BF16)


def twist_of(steps):
    parts = steps[2 * LANES :].astype(F32)
    turns = parts[:, : 2 * LANES] + parts[:, 2 * LANES : 4 * LANES]
    return turns[:, :LANES], turns[:, LANES:]


def to_spectrum(grid_ref, turned_ref, steps):
    first = steps[: 2 * BLOCKS, 4 * LANES : 4 * LANES + BLOCKS]
    cos_twist, sin_twist = twist_of(steps)
    for c in range(CHANNELS):
        grid = grid_ref[pl.ds(c, BLOCKS, stride=CHANNELS), :].astype(BF16)
        section = jnp.dot(first, grid, preferred_element_type=F32)
        real, imag = section[:BLOCKS], section[BLOCKS:]
        rows = slice(c * BLOCKS, (c + 1) * BLOCKS)
        turned_ref[rows, :LANES] = (real * cos_twist + imag * sin_twist).astype(BF16)
        turned_ref[rows, LANES:] = (imag * cos_twist - real * sin_twist).astype(BF16)
    return jnp.dot(turned_ref[...], steps[: 2 * LANES, : 2 * LANES], preferred_element_type=F32)


def from_spectrum(spectrum, grid_ref, section_ref, steps):
    first_back = steps[2 * BLOCKS : 3 * BLOCKS, 4 * LANES : 4 * LANES + 2 * BLOCKS]
    cos_twist, sin_twist = twist_of(steps)
    section_ref[...] = jnp.dot(
        spectrum, steps[: 2 * LANES, 2 * LANES : 4 * LANES], preferred_element_type=F32
    )
    for c in range(CHANNELS):
        rows = slice(c * BLOCKS, (c + 1) * BLOCKS)
        real, imag = section_ref[rows, :LANES], section_ref[rows, LANES:]
        turned = jnp.concatenate(
            [real * cos_twist - imag * sin_twist, imag * cos_twist + real * sin_twist], axis=0
        ).astype(BF16)
        grid_ref[pl.ds(c, BLOCKS, stride=CHANNELS), :] = jnp.dot(
            first_back, turned, preferred_element_type=F32
        )


def filter_kernel(filter_ref, steps, spectrum_ref, grid, turned):
    for b in range(BLOCKS):
        grid[b * CHANNELS : (b + 1) * CHANNELS, :] = filter_ref[:, b * LANES : (b + 1) * LANES]
    spectrum_ref[...] = to_spectrum(grid, turned, steps).astype(BF16)


def forward_kernel(
    product_ref, filter_spectrum, steps, long_ref, product_spectrum, grid, turned, section
):
    grid[:ROWS] = product_ref[...].astype(F32).reshape(ROWS, LANES)
    own = to_spectrum(grid, turned, steps)
    product_spectrum[...] = own.astype(BF16)
    own_re, own_im = own[:, :LANES], own[:, LANES:]
    other = filter_spectrum[...].astype(F32)
    other_re, other_im = other[:, :LANES], other[:, LANES:]
    turned[:, :LANES] = (own_re * other_re - own_im * other_im).astype(BF16)
    turned[:, LANES:] = (own_re * other_im + own_im * other_re).astype(BF16)
    from_spectrum(turned[...], grid, section, steps)
    long_ref[...] = grid[:ROWS].reshape(BLOCKS, CHANNELS, LANES).astype(BF16)


def correlate(grad_ref, other, grid, turned, section, steps):
    grid[:ROWS] = grad_ref[...].astype(F32).reshape(ROWS, LANES)
    own = to_spectrum(grid, turned, steps)
    own_re, own_im = own[:, :LANES], own[:, LANES:]
    other_re, other_im = other[:, :LANES].astype(F32), other[:, LANES:].astype(F32)
    turned[:, :LANES] = (own_re * other_re + own_im * other_im).astype(BF16)
    turned[:, LANES:] = (own_im * other_re - own_re * other_im).astype(BF16)
    from_spectrum(turned[...], grid, section, steps)


def backward_kernel(grad_ref, filter_spectrum, steps, back_ref, grid, turned, section):
    correlate(grad_ref, filter_spectrum, grid, turned, section, steps)
    back_ref[...] = grid[:ROWS].reshape(BLOCKS, CHANNELS, LANES).astype(BF16)


def filter_grad_kernel(
    grad_ref, product_spectrum, steps, _, filter_grad_ref, grid, turned, section
):
    correlate(grad_ref, product_spectrum, grid, turned, section, steps)
    for b in range(BLOCKS):
        filter_grad_ref[:, b * LANES : (b + 1) * LANES] = grid[
            b * CHANNELS : (b + 1) * CHANNELS, :
        ] * (1.0 / math.sqrt(LENGTH))


SPECTRUM = jax.ShapeDtypeStruct((CHANNELS * BLOCKS, 2 * LANES), BF16)
SEQUENCES = jax.ShapeDtypeStruct((BLOCKS, CHANNELS, LANES), BF16)
GRID = pltpu.VMEM((ROWS + CHANNELS, LANES), F32)
TURNED = pltpu.VMEM((CHANNELS * BLOCKS, 2 * LANES), BF16)
SECTION = pltpu.VMEM((CHANNELS * BLOCKS, 2 * LANES), F32)


def run_kernel(kernel, out_shape, scratch, transforms, *operands, unread=()):
    in_specs = [
        pl.BlockSpec(memory_space=pl.ANY if i in unread else pltpu.VMEM) for i in range(len(operands))
    ]
    transform_flops = 2 * CHANNELS * BLOCKS * LANES * (2 * BLOCKS + 4 * LANES)
    return pl.pallas_call(
        kernel,
        out_shape=out_shape,
        in_specs=in_specs,
        scratch_shapes=scratch,
        compiler_params=pltpu.CompilerParams(vmem_limit_bytes=VMEM_LIMIT),
        cost_estimate=pl.CostEstimate(
            flops=transforms * transform_flops, bytes_accessed=4 * 2**20, transcendentals=0
        ),
    )(*operands)


def run_blocks(kernel, steps, ins, outs, moved, flops=10**6, scratch=(), limit=VMEM_LIMIT, pinned=False, alias=()):
    def spec(block, axis):
        if block is None:
            return pl.BlockSpec(memory_space=axis or pl.ANY)
        fixed = (0,) * len(block)
        if isinstance(block[0], tuple):
            block, fixed = block
        return pl.BlockSpec(block, lambda i: tuple(i if d == axis else fixed[d] for d in range(len(block))))

    return pl.pallas_call(
        kernel,
        grid=(steps,),
        in_specs=[spec(block, axis) for _, block, axis in ins],
        out_specs=[spec(block, axis) for _, _, block, axis in outs],
        out_shape=[
            (pltpu.HBM if pinned else jax.ShapeDtypeStruct)(shape, dtype) for shape, dtype, _, _ in outs
        ],
        input_output_aliases=dict(alias),
        scratch_shapes=list(scratch),
        compiler_params=pltpu.CompilerParams(vmem_limit_bytes=limit),
        cost_estimate=pl.CostEstimate(flops=flops, bytes_accessed=moved, transcendentals=0),
    )(*[array for array, _, _ in ins])


def row_numbers(value):
    return lax.broadcasted_iota(jnp.int32, value.shape, 0)


def causal(value, before, taps):
    number = row_numbers(value)
    one = jnp.where(number == 0, before[1:2], pltpu.roll(value, 1, 0))
    two = jnp.where(number == 0, before[0:1], pltpu.roll(value, 2, 0))
    two = jnp.where(number == 1, before[1:2], two)
    return taps[0:1] * value + taps[1:2] * one + taps[2:3] * two


def adjoint(value, after, taps):
    rows = value.shape[0]
    number = row_numbers(value)
    one = jnp.where(number == rows - 1, after[0:1], pltpu.roll(value, rows - 1, 0))
    two = jnp.where(number == rows - 1, after[1:2], pltpu.roll(value, rows - 2, 0))
    two = jnp.where(number == rows - 2, after[0:1], two)
    return taps[0:1] * value + taps[1:2] * one + taps[2:3] * two


def filter_product(k_ref, v_ref, before_ref, taps_ref, product_ref):
    kc = causal(k_ref[...].astype(F32), before_ref[1].astype(F32), taps_ref[1])
    vc = causal(v_ref[...].astype(F32), before_ref[2].astype(F32), taps_ref[2])
    product_ref[...] = (kc * vc).T.astype(BF16)


def filter_inputs(
    q_ref, k_ref, v_ref, before_ref, taps_ref, _, qc_ref, kc_ref, vc_ref, turned_ref
):
    sources, results = (q_ref, k_ref, v_ref), (qc_ref, kc_ref, vc_ref)
    for i in range(3):
        results[i][...] = causal(sources[i][...].astype(F32), before_ref[i].astype(F32), taps_ref[i])
    turned_ref[...] = qc_ref[...].T


def gate(long_ref, qc_ref, gated_ref):
    gated = (qc_ref[...] * long_ref[...].astype(F32).T).astype(BF16)
    for co in range(2):
        for y in range(4):
            start = (2 * (y % 2) + co) * LANES
            gated_ref[co, y] = gated[:, start : start + LANES]


def partial_kernel(place_ref, gradient_ref, weight_ref, _, out_ref, total):
    xh, xl, yl = place_ref[0], place_ref[1], place_ref[3]
    step = pl.program_id(0)
    features, tokens = gradient_ref.shape[2:]
    rows = tokens // 2
    added = jnp.dot(
        weight_ref[...].reshape(total.shape[0], features),
        gradient_ref[(step // 2) ^ yl, (step % 2) ^ xl],
        preferred_element_type=F32,
    )

    @pl.when(step == 0)
    def _():
        total[...] = added

    @pl.when(step > 0)
    def _():
        total[...] += added

    @pl.when(step == pl.num_programs(0) - 1)
    def _():
        for t in range(2):
            value = total[:, t * rows : (t + 1) * rows].astype(BF16)
            out_ref[t ^ xh] = value.reshape(out_ref.shape[1:])


def long_gradient(parts_ref, qc_ref, long_ref, grad_ref, qg_ref):
    for e in range(2):
        for r in range(2):
            rows = slice((2 * e + r) * LANES, (2 * e + r + 1) * LANES)
            gated_grad = parts_ref[4 * r + e].astype(F32) + parts_ref[4 * r + 2 + e].astype(F32)
            grad_ref[rows] = (qc_ref[rows] * gated_grad).astype(BF16)
            qg_ref[rows] = gated_grad * long_ref[rows].astype(F32)


def mix_kernel(gated_ref, weight_ref, out_ref, total):
    halves, _, rows, width = gated_ref.shape
    features = weight_ref.shape[4]
    step = pl.program_id(0)

    @pl.when(step == 0)
    def _():
        total[...] = jnp.zeros_like(total)

    gated = gated_ref[...].reshape(halves * rows, width)
    for e in range(2):
        for f in range(2):
            total[2 * e + f] += jnp.dot(
                gated, weight_ref[0, :, 2 * e + f].reshape(width, features), preferred_element_type=F32
            )

    @pl.when(step == pl.num_programs(0) - 1)
    def _():
        for e in range(2):
            for f in range(2):
                for t in range(2):
                    out_ref[t, f, e] = total[2 * e + f, t * rows : (t + 1) * rows].astype(BF16)


def query_adjoint(qg_ref, after_ref, taps_ref, out_ref):
    out_ref[...] = adjoint(qg_ref[...].T, after_ref[...], taps_ref[0]).astype(BF16)


def key_value_adjoint(back_ref, kc_ref, vc_ref, taps_ref, key_ref, value_ref):
    back = back_ref[...].astype(F32).T
    after = jnp.zeros((2, back.shape[1]), F32)
    key_ref[...] = adjoint(back * vc_ref[...], after, taps_ref[1]).astype(BF16)
    value_ref[...] = adjoint(back * kc_ref[...], after, taps_ref[2]).astype(BF16)


def key_value_rim(
    tail_ref, kc_ref, vc_ref, after_ref, next_ref, taps_ref, _, __, key_ref, value_ref
):
    back = tail_ref[...].astype(F32)
    after = after_ref[...].astype(F32)
    key_ref[...] = adjoint(back * vc_ref[...], after * next_ref[1], taps_ref[1]).astype(BF16)
    value_ref[...] = adjoint(back * kc_ref[...], after * next_ref[0], taps_ref[2]).astype(BF16)


def shift(value, steps):
    count = 1
    for axis in SEQ:
        count *= lax.axis_size(axis)
    first, last = max(0, -steps), min(count, count - steps)
    return lax.ppermute(value, SEQ, [(i, i + steps) for i in range(first, last)])


def partner(value, axis):
    return lax.ppermute(value, axis, [(0, 1), (1, 0)])


def across(value, dx, dl):
    if not (dx or dl):
        return value
    return lax.ppermute(value, ("xh", "xl"), [(i, i ^ (2 * dx + dl)) for i in range(4)])


def turn(value):
    pairs = []
    for i in range(32):
        a, s, c, b, e = ((i >> k) & 1 for k in (4, 3, 2, 1, 0))
        pairs.append((i, 16 * c + 8 * e + 4 * b + 2 * a + s))
    return lax.ppermute(value, ("xh", "zb", "co", "xl", "yl"), pairs)


def per_device(queries, keys, values, short_taps, long_filter, out_weight, cotangent):
    rows, width = queries.shape
    features = out_weight.shape[1]
    place = jnp.stack([lax.axis_index(axis) for axis in ("xh", "xl", "yh", "yl")])
    place = (place.astype(jnp.int32), None, pltpu.SMEM)
    kinds, chunk = 4, width // 4

    rims = jnp.stack([x[rows - 2 :] for x in (queries, keys, values)])
    rims, out_weight = lax.optimization_barrier((rims, out_weight))
    before, turned = lax.optimization_barrier((shift(rims, 1), turn(out_weight)))
    weight = lax.all_gather(turned, COLUMN, axis=0).reshape(4, 2, 4, rows, features)
    weight = pltpu.with_memory_space_constraint(weight, pltpu.HBM)

    steps = transform_tables()
    filter_spectrum = run_kernel(filter_kernel, SPECTRUM, [GRID, TURNED], 1, long_filter, steps)

    tokens = (rows, chunk)
    channels = (chunk, rows)
    taps_block = (3, 3, chunk)
    plane = ((rows, width), F32, tokens, 1)
    (product,) = run_blocks(
        filter_product, 1,
        [(keys, (rows, width), 1), (values, (rows, width), 1), (before, before.shape, 2), (short_taps, short_taps.shape, 2)],
        [((width, rows), BF16, (width, rows), 0)], 2**20, limit=WHOLE_VMEM,
    )
    query_conv, key_conv, value_conv, query_turned = run_blocks(
        filter_inputs, kinds,
        [(queries, tokens, 1), (keys, tokens, 1), (values, tokens, 1),
         (before, (3, 2, chunk), 2), (short_taps, taps_block, 2), (product, None, None)],
        [plane, plane, plane, ((width, rows), F32, channels, 0)], 3 * 2**20, limit=WHOLE_VMEM,
    )

    product_owned = lax.all_to_all(product.reshape(BLOCKS, CHANNELS, LANES), SEQ, 0, 0, tiled=True)
    long_owned, product_spectrum = run_kernel(
        forward_kernel, [pltpu.HBM(SEQUENCES.shape, BF16), pltpu.HBM(SPECTRUM.shape, BF16)], [GRID, TURNED, SECTION], 2,
        product_owned, filter_spectrum, steps,
    )
    turned = cotangent.T
    gradient = jnp.stack(
        [jnp.concatenate([across(turned, dx, dl) for dx in range(2)], axis=1) for dl in range(2)]
    )
    gradient = jnp.stack([gradient, partner(gradient, "yl")])

    long_raw = lax.all_to_all(long_owned, SEQ, 0, 0, tiled=True).reshape(width, rows)
    wide, tall = (rows, width // 2), (width // 2, rows)

    (gated,) = run_blocks(
        gate, 2,
        [(long_raw, tall, 0), (query_conv, wide, 1)],
        [((2, 4, rows, chunk), BF16, (2, 4, rows, LANES), 3)], 2 * 2**20, pinned=True,
    )

    mixing = lax.all_to_all(gated.reshape(8, rows, chunk), PLANE, 0, 0, tiled=True)

    (partial,) = run_blocks(
        partial_kernel, kinds,
        [place, (gradient, gradient.shape, None),
         (weight, (4, 2, 1, rows, features), 2), (mixing, None, None)],
        [((2, 4, chunk, rows), BF16, (2, 4, chunk, rows), None)], 6 * 2**20, 2**30,
        [pltpu.VMEM((width, 2 * rows), F32)],
    )
    arrived = lax.all_to_all(partial.reshape(8, chunk, rows), PLANE, 0, 0, tiled=True)
    long_grad, query_conv_grad = run_blocks(
        long_gradient, 2,
        [(arrived, (8, LANES, rows), 1), (query_turned, tall, 0), (long_raw, tall, 0)],
        [((width, rows), BF16, tall, 0), ((width, rows), F32, tall, 0)], 3 * 2**20, pinned=True,
    )
    grad_owned = lax.all_to_all(long_grad.reshape(BLOCKS, CHANNELS, LANES), SEQ, 0, 0, tiled=True)

    back_owned = run_kernel(
        backward_kernel, pltpu.HBM(SEQUENCES.shape, BF16), [GRID, TURNED, SECTION], 2,
        grad_owned, filter_spectrum, steps,
    )
    filter_grad = run_kernel(
        filter_grad_kernel, jax.ShapeDtypeStruct((CHANNELS, LENGTH), F32), [GRID, TURNED, SECTION], 2,
        grad_owned, product_spectrum, steps, back_owned, unread=(3,),
    )

    quarter = (1, 2, 4, rows, features)
    (share,) = run_blocks(
        mix_kernel, kinds,
        [(mixing.reshape(2, 4, rows, chunk), (2, 1, rows, chunk), 1), (weight, quarter, 0)],
        [((2, 2, 2, rows, features), BF16, (2, 2, 2, rows, features), None)], 6 * 2**20, 2**30,
        [pltpu.VMEM((4, 2 * rows, features), F32)],
    )
    mixed = lax.psum_scatter(
        share.reshape(8 * rows, features), ("xh", "xl", "yl"), scatter_dimension=0, tiled=True
    )

    rim = (2, chunk)
    (query_grad,) = run_blocks(
        query_adjoint, kinds,
        [(query_conv_grad, channels, 0), (shift(query_conv_grad[:, :2].T, -1), rim, 1), (short_taps, taps_block, 2)],
        [((rows, width), BF16, tokens, 1)], 2**20,
    )
    following = shift(jnp.stack([key_conv[:2], value_conv[:2]]), -1)

    back_raw = lax.all_to_all(back_owned, SEQ, 0, 0, tiled=True).reshape(width, rows)
    head, query_grad, filter_grad = lax.optimization_barrier((back_raw[:, :2].T, query_grad, filter_grad))
    after = shift(head, -1)
    grads = run_blocks(
        key_value_adjoint, kinds,
        [(back_raw, channels, 0), (key_conv, tokens, 1), (value_conv, tokens, 1), (short_taps, taps_block, 2)],
        [((rows, width), BF16, tokens, 1)] * 2, 3 * 2**20,
    )
    tail = (RIM, width)
    last = (tail, (rows // RIM - 1, 0))
    key_grad, value_grad = run_blocks(
        key_value_rim, 1,
        [(back_raw[:, rows - RIM :].T, tail, None), (key_conv, last, None), (value_conv, last, None),
         (after, (2, width), None), (following, (2, 2, width), None), (short_taps, (3, 3, width), None),
         (grads[0], None, None), (grads[1], None, None)],
        [((rows, width), BF16, last, None)] * 2, 2**20, alias=((6, 0), (7, 1)),
    )
    return (mixed, query_grad, key_grad, value_grad, filter_grad)


def solution(mesh):
    fine = Mesh(mesh.devices.reshape(tuple(AXES.values())), tuple(AXES))
    token = P(SEQ, TP)
    in_specs = (token, token, token, P(None, None, TP), P(TP + SEQ, None), token, token)
    out_specs = (token, token, token, token, P(TP + SEQ, None))
    return jax.shard_map(
        per_device, mesh=fine, in_specs=in_specs, out_specs=out_specs, check_vma=False
    )
```

```python
import math

import jax
import jax.numpy as jnp
import numpy as np
from jax import lax
from jax.experimental import pallas as pl
from jax.experimental.pallas import tpu as pltpu
from jax.sharding import Mesh
from jax.sharding import PartitionSpec as P

BF16 = jnp.bfloat16
F32 = jnp.float32

AXES = {"xh": 2, "zy": 4, "zh": 2, "zb": 2, "co": 2, "xl": 2, "yh": 2, "yl": 2}
SEQ = ("xh", "zy", "zh", "zb", "co")
TP = ("xl", "yh", "yl")
PLANE = ("xh", "yh", "yl")
COLUMN = ("zy", "zh", "zb", "co")

CHANNELS = 16
BLOCKS = 64
LANES = 128
LENGTH = BLOCKS * LANES
ROWS = BLOCKS * CHANNELS

RIM = 16
VMEM_LIMIT = 20 * 2**20
WHOLE_VMEM = 60 * 2**20


def transform_tables():
    blocks = np.arange(BLOCKS)
    lanes = np.arange(LANES)
    first = 2.0 * np.pi * np.outer(blocks + 0.25, blocks) / BLOCKS
    twist = 2.0 * np.pi * np.outer(blocks + 0.25, lanes) / LENGTH
    second = 2.0 * np.pi * (np.outer(lanes, lanes) % LANES) / LANES
    first_table = np.concatenate([np.cos(first), -np.sin(first)], axis=0)
    cosine, sine = np.cos(second), np.sin(second)
    second_table = np.block([[cosine, -sine], [sine, cosine]])
    steps = np.zeros((2 * LANES + BLOCKS, 5 * LANES))
    steps[: 2 * LANES, : 2 * LANES] = second_table
    steps[: 2 * LANES, 2 * LANES : 4 * LANES] = second_table.T
    steps[: 2 * BLOCKS, 4 * LANES : 4 * LANES + BLOCKS] = first_table
    steps[2 * BLOCKS : 3 * BLOCKS, 4 * LANES : 4 * LANES + 2 * BLOCKS] = first_table.T / LENGTH
    turns = np.concatenate([np.cos(twist), np.sin(twist)], axis=1)
    coarse = turns.astype(BF16).astype(np.float64)
    steps[2 * LANES :, : 2 * LANES] = coarse
    steps[2 * LANES :, 2 * LANES : 4 * LANES] = turns - coarse
    return jnp.asarray(steps, BF16)


def twist_of(steps):
    parts = steps[2 * LANES :].astype(F32)
    turns = parts[:, : 2 * LANES] + parts[:, 2 * LANES : 4 * LANES]
    return turns[:, :LANES], turns[:, LANES:]


def to_spectrum(grid_ref, turned_ref, steps):
    first = steps[: 2 * BLOCKS, 4 * LANES : 4 * LANES + BLOCKS]
    cos_twist, sin_twist = twist_of(steps)
    for c in range(CHANNELS):
        grid = grid_ref[pl.ds(c, BLOCKS, stride=CHANNELS), :].astype(BF16)
        section = jnp.dot(first, grid, preferred_element_type=F32)
        real, imag = section[:BLOCKS], section[BLOCKS:]
        rows = slice(c * BLOCKS, (c + 1) * BLOCKS)
        turned_ref[rows, :LANES] = (real * cos_twist + imag * sin_twist).astype(BF16)
        turned_ref[rows, LANES:] = (imag * cos_twist - real * sin_twist).astype(BF16)
    return jnp.dot(turned_ref[...], steps[: 2 * LANES, : 2 * LANES], preferred_element_type=F32)


def from_spectrum(spectrum, grid_ref, section_ref, steps):
    first_back = steps[2 * BLOCKS : 3 * BLOCKS, 4 * LANES : 4 * LANES + 2 * BLOCKS]
    cos_twist, sin_twist = twist_of(steps)
    section_ref[...] = jnp.dot(
        spectrum, steps[: 2 * LANES, 2 * LANES : 4 * LANES], preferred_element_type=F32
    )
    for c in range(CHANNELS):
        rows = slice(c * BLOCKS, (c + 1) * BLOCKS)
        real, imag = section_ref[rows, :LANES], section_ref[rows, LANES:]
        turned = jnp.concatenate(
            [real * cos_twist - imag * sin_twist, imag * cos_twist + real * sin_twist], axis=0
        ).astype(BF16)
        grid_ref[pl.ds(c, BLOCKS, stride=CHANNELS), :] = jnp.dot(
            first_back, turned, preferred_element_type=F32
        )


def filter_kernel(filter_ref, steps, spectrum_ref, kept_ref, grid, turned):
    kept_ref[...] = steps[...]
    for b in range(BLOCKS):
        grid[b * CHANNELS : (b + 1) * CHANNELS, :] = filter_ref[:, b * LANES : (b + 1) * LANES]
    spectrum_ref[...] = to_spectrum(grid, turned, steps).astype(BF16)


def forward_kernel(
    product_ref, filter_spectrum, steps, long_ref, product_spectrum, grid, turned, section
):
    grid[:ROWS] = product_ref[...].astype(F32).reshape(ROWS, LANES)
    own = to_spectrum(grid, turned, steps)
    product_spectrum[...] = own.astype(BF16)
    own_re, own_im = own[:, :LANES], own[:, LANES:]
    other = filter_spectrum[...].astype(F32)
    other_re, other_im = other[:, :LANES], other[:, LANES:]
    turned[:, :LANES] = (own_re * other_re - own_im * other_im).astype(BF16)
    turned[:, LANES:] = (own_re * other_im + own_im * other_re).astype(BF16)
    from_spectrum(turned[...], grid, section, steps)
    long_ref[...] = grid[:ROWS].reshape(BLOCKS, CHANNELS, LANES).astype(BF16)


def correlate(grad_ref, other, grid, turned, section, steps, fetch=None):
    grid[:ROWS] = grad_ref[...].astype(F32).reshape(ROWS, LANES)
    own = to_spectrum(grid, turned, steps)
    own_re, own_im = own[:, :LANES], own[:, LANES:]
    if fetch is not None:
        fetch.wait()
    other_re, other_im = other[:, :LANES].astype(F32), other[:, LANES:].astype(F32)
    turned[:, :LANES] = (own_re * other_re + own_im * other_im).astype(BF16)
    turned[:, LANES:] = (own_im * other_re - own_re * other_im).astype(BF16)
    from_spectrum(turned[...], grid, section, steps)


def backward_kernel(
    grad_ref, spectrum_ref, steps, back_ref, grid, turned, section, filter_spectrum, fetched
):
    fetch = pltpu.make_async_copy(spectrum_ref, filter_spectrum, fetched)
    fetch.start()
    correlate(grad_ref, filter_spectrum, grid, turned, section, steps, fetch)
    back_ref[...] = grid[:ROWS].reshape(BLOCKS, CHANNELS, LANES).astype(BF16)


def filter_grad_kernel(
    grad_ref, product_spectrum, steps, _, filter_grad_ref, grid, turned, section
):
    correlate(grad_ref, product_spectrum, grid, turned, section, steps)
    for b in range(BLOCKS):
        filter_grad_ref[:, b * LANES : (b + 1) * LANES] = grid[
            b * CHANNELS : (b + 1) * CHANNELS, :
        ] * (1.0 / math.sqrt(LENGTH))


SPECTRUM = jax.ShapeDtypeStruct((CHANNELS * BLOCKS, 2 * LANES), BF16)
SEQUENCES = jax.ShapeDtypeStruct((BLOCKS, CHANNELS, LANES), BF16)
GRID = pltpu.VMEM((ROWS + CHANNELS, LANES), F32)
TURNED = pltpu.VMEM((CHANNELS * BLOCKS, 2 * LANES), BF16)
SECTION = pltpu.VMEM((CHANNELS * BLOCKS, 2 * LANES), F32)


def run_kernel(kernel, out_shape, scratch, transforms, *operands, unread=()):
    in_specs = [
        pl.BlockSpec(memory_space=pl.ANY if i in unread else pltpu.VMEM) for i in range(len(operands))
    ]
    transform_flops = 2 * CHANNELS * BLOCKS * LANES * (2 * BLOCKS + 4 * LANES)
    return pl.pallas_call(
        kernel,
        out_shape=out_shape,
        in_specs=in_specs,
        scratch_shapes=scratch,
        compiler_params=pltpu.CompilerParams(vmem_limit_bytes=VMEM_LIMIT),
        cost_estimate=pl.CostEstimate(
            flops=transforms * transform_flops, bytes_accessed=4 * 2**20, transcendentals=0
        ),
    )(*operands)


def run_blocks(kernel, steps, ins, outs, moved, flops=10**6, scratch=(), limit=VMEM_LIMIT, pinned=False, alias=()):
    def spec(block, axis):
        if block is None:
            return pl.BlockSpec(memory_space=axis or pl.ANY)
        fixed = (0,) * len(block)
        if isinstance(block[0], tuple):
            block, fixed = block
        return pl.BlockSpec(block, lambda i: tuple(i if d == axis else fixed[d] for d in range(len(block))))

    return pl.pallas_call(
        kernel,
        grid=(steps,),
        in_specs=[spec(block, axis) for _, block, axis in ins],
        out_specs=[spec(block, axis) for _, _, block, axis in outs],
        out_shape=[
            (pltpu.HBM if pinned else jax.ShapeDtypeStruct)(shape, dtype) for shape, dtype, _, _ in outs
        ],
        input_output_aliases=dict(alias),
        scratch_shapes=list(scratch),
        compiler_params=pltpu.CompilerParams(vmem_limit_bytes=limit),
        cost_estimate=pl.CostEstimate(flops=flops, bytes_accessed=moved, transcendentals=0),
    )(*[array for array, _, _ in ins])


def row_numbers(value):
    return lax.broadcasted_iota(jnp.int32, value.shape, 0)


def causal(value, before, taps):
    number = row_numbers(value)
    one = jnp.where(number == 0, before[1:2], pltpu.roll(value, 1, 0))
    two = jnp.where(number == 0, before[0:1], pltpu.roll(value, 2, 0))
    two = jnp.where(number == 1, before[1:2], two)
    return taps[0:1] * value + taps[1:2] * one + taps[2:3] * two


def adjoint(value, after, taps):
    rows = value.shape[0]
    number = row_numbers(value)
    one = jnp.where(number == rows - 1, after[0:1], pltpu.roll(value, rows - 1, 0))
    two = jnp.where(number == rows - 1, after[1:2], pltpu.roll(value, rows - 2, 0))
    two = jnp.where(number == rows - 2, after[0:1], two)
    return taps[0:1] * value + taps[1:2] * one + taps[2:3] * two


def filter_product(k_ref, v_ref, before_ref, taps_ref, product_ref):
    kc = causal(k_ref[...].astype(F32), before_ref[1].astype(F32), taps_ref[1])
    vc = causal(v_ref[...].astype(F32), before_ref[2].astype(F32), taps_ref[2])
    product_ref[...] = (kc * vc).T.astype(BF16)


def filter_inputs(
    q_ref, k_ref, v_ref, before_ref, taps_ref, _, qc_ref, kc_ref, vc_ref, turned_ref
):
    sources, results = (q_ref, k_ref, v_ref), (qc_ref, kc_ref, vc_ref)
    for i in range(3):
        results[i][...] = causal(sources[i][...].astype(F32), before_ref[i].astype(F32), taps_ref[i])
    turned_ref[...] = qc_ref[...].T


def gate(long_ref, qc_ref, gated_ref):
    gated = (qc_ref[...] * long_ref[...].astype(F32).T).astype(BF16)
    for co in range(2):
        for y in range(4):
            start = (2 * (y % 2) + co) * LANES
            gated_ref[co, y] = gated[:, start : start + LANES]


def partial_kernel(place_ref, gradient_ref, weight_ref, _, out_ref):
    xh, xl, yl = place_ref[0], place_ref[1], place_ref[3]
    kinds, features, tokens = weight_ref.shape[2], *gradient_ref.shape[2:]
    rows = tokens // 2
    for zy in range(weight_ref.shape[0]):
        total = jnp.zeros((out_ref.shape[2], tokens), F32)
        for k in range(kinds):
            total += jnp.dot(
                weight_ref[zy, :, k].reshape(-1, features),
                gradient_ref[(k // 2) ^ yl, (k % 2) ^ xl],
                preferred_element_type=F32,
            )
        total = total.astype(BF16)
        for t in range(2):
            out_ref[t ^ xh, zy] = total[:, t * rows : (t + 1) * rows]


def long_gradient(parts_ref, qc_ref, long_ref, grad_ref, qg_ref):
    for e in range(2):
        for r in range(2):
            rows = slice((2 * e + r) * LANES, (2 * e + r + 1) * LANES)
            gated_grad = parts_ref[4 * r + e].astype(F32) + parts_ref[4 * r + 2 + e].astype(F32)
            grad_ref[rows] = (qc_ref[rows] * gated_grad).astype(BF16)
            qg_ref[rows] = gated_grad * long_ref[rows].astype(F32)


def mix_kernel(gated_ref, weight_ref, out_ref, total):
    halves, _, rows, width = gated_ref.shape
    features = weight_ref.shape[4]
    step = pl.program_id(0)

    @pl.when(step == 0)
    def _():
        total[...] = jnp.zeros_like(total)

    gated = gated_ref[...].reshape(halves * rows, width)
    for e in range(2):
        for f in range(2):
            total[2 * e + f] += jnp.dot(
                gated, weight_ref[0, :, 2 * e + f].reshape(width, features), preferred_element_type=F32
            )

    @pl.when(step == pl.num_programs(0) - 1)
    def _():
        for e in range(2):
            for f in range(2):
                for t in range(2):
                    out_ref[t, f, e] = total[2 * e + f, t * rows : (t + 1) * rows].astype(BF16)


def query_adjoint(qg_ref, after_ref, taps_ref, out_ref):
    out_ref[...] = adjoint(qg_ref[...].T, after_ref[...], taps_ref[0]).astype(BF16)


def key_value_adjoint(back_ref, kc_ref, vc_ref, taps_ref, key_ref, value_ref):
    back = back_ref[...].astype(F32).T
    after = jnp.zeros((2, back.shape[1]), F32)
    key_ref[...] = adjoint(back * vc_ref[...], after, taps_ref[1]).astype(BF16)
    value_ref[...] = adjoint(back * kc_ref[...], after, taps_ref[2]).astype(BF16)


def key_value_rim(
    tail_ref, kc_ref, vc_ref, after_ref, next_ref, taps_ref, _, __, key_ref, value_ref
):
    back = tail_ref[...].astype(F32)
    after = after_ref[...].astype(F32)
    key_ref[...] = adjoint(back * vc_ref[...], after * next_ref[1], taps_ref[1]).astype(BF16)
    value_ref[...] = adjoint(back * kc_ref[...], after * next_ref[0], taps_ref[2]).astype(BF16)


def shift(value, steps):
    count = 1
    for axis in SEQ:
        count *= lax.axis_size(axis)
    first, last = max(0, -steps), min(count, count - steps)
    return lax.ppermute(value, SEQ, [(i, i + steps) for i in range(first, last)])


def partner(value, axis):
    return lax.ppermute(value, axis, [(0, 1), (1, 0)])


def across(value, dx, dl):
    if not (dx or dl):
        return value
    return lax.ppermute(value, ("xh", "xl"), [(i, i ^ (2 * dx + dl)) for i in range(4)])


def turn(value):
    pairs = []
    for i in range(32):
        a, s, c, b, e = ((i >> k) & 1 for k in (4, 3, 2, 1, 0))
        pairs.append((i, 16 * c + 8 * e + 4 * b + 2 * a + s))
    return lax.ppermute(value, ("xh", "zb", "co", "xl", "yl"), pairs)


def per_device(queries, keys, values, short_taps, long_filter, out_weight, cotangent):
    rows, width = queries.shape
    features = out_weight.shape[1]
    place = jnp.stack([lax.axis_index(axis) for axis in ("xh", "xl", "yh", "yl")])
    place = (place.astype(jnp.int32), None, pltpu.SMEM)
    kinds, chunk = 4, width // 4

    rims = jnp.stack([x[rows - 2 :] for x in (queries, keys, values)])
    rims, out_weight = lax.optimization_barrier((rims, out_weight))
    before, turned = lax.optimization_barrier((shift(rims, 1), turn(out_weight)))
    weight = lax.all_gather(turned, COLUMN, axis=0).reshape(4, 2, 4, rows, features)

    steps = transform_tables()
    kept = jax.ShapeDtypeStruct(steps.shape, BF16)
    filter_spectrum, kept = run_kernel(
        filter_kernel, [SPECTRUM, kept], [GRID, TURNED], 1, long_filter, steps
    )

    tokens = (rows, chunk)
    channels = (chunk, rows)
    taps_block = (3, 3, chunk)
    plane = ((rows, width), F32, tokens, 1)
    (product,) = run_blocks(
        filter_product, 1,
        [(keys, (rows, width), 1), (values, (rows, width), 1), (before, before.shape, 2), (short_taps, short_taps.shape, 2)],
        [((width, rows), BF16, (width, rows), 0)], 2**20, limit=WHOLE_VMEM,
    )
    query_conv, key_conv, value_conv, query_turned = run_blocks(
        filter_inputs, kinds,
        [(queries, tokens, 1), (keys, tokens, 1), (values, tokens, 1),
         (before, (3, 2, chunk), 2), (short_taps, taps_block, 2), (product, None, None)],
        [plane, plane, plane, ((width, rows), F32, channels, 0)], 3 * 2**20,
    )

    product_owned = lax.all_to_all(product.reshape(BLOCKS, CHANNELS, LANES), SEQ, 0, 0, tiled=True)
    long_owned, product_spectrum = run_kernel(
        forward_kernel, [pltpu.HBM(SEQUENCES.shape, BF16), pltpu.HBM(SPECTRUM.shape, BF16)], [GRID, TURNED, SECTION], 2,
        product_owned, filter_spectrum, kept,
    )
    turned = cotangent.T
    gradient = jnp.stack(
        [jnp.concatenate([across(turned, dx, dl) for dx in range(2)], axis=1) for dl in range(2)]
    )
    gradient = jnp.stack([gradient, partner(gradient, "yl")])

    long_raw = lax.all_to_all(long_owned, SEQ, 0, 0, tiled=True).reshape(width, rows)
    wide, tall = (rows, width // 2), (width // 2, rows)

    (gated,) = run_blocks(
        gate, 2,
        [(long_raw, tall, 0), (query_conv, wide, 1)],
        [((2, 4, rows, chunk), BF16, (2, 4, rows, LANES), 3)], 2 * 2**20, pinned=True,
    )

    mixing = lax.all_to_all(gated.reshape(8, rows, chunk), PLANE, 0, 0, tiled=True)

    memory = (pltpu.SMEM, pltpu.VMEM, pltpu.VMEM, pl.ANY)
    partial = pl.pallas_call(
        partial_kernel,
        in_specs=[pl.BlockSpec(memory_space=space) for space in memory],
        out_shape=jax.ShapeDtypeStruct((2, 4, chunk, rows), BF16),
        compiler_params=pltpu.CompilerParams(vmem_limit_bytes=VMEM_LIMIT),
        cost_estimate=pl.CostEstimate(flops=2**30, bytes_accessed=6 * 2**20, transcendentals=0),
    )(place[0], gradient, weight, mixing)
    arrived = lax.all_to_all(partial.reshape(8, chunk, rows), PLANE, 0, 0, tiled=True)
    long_grad, query_conv_grad = run_blocks(
        long_gradient, 2,
        [(arrived, (8, LANES, rows), 1), (query_turned, tall, 0), (long_raw, tall, 0)],
        [((width, rows), BF16, tall, 0), ((width, rows), F32, tall, 0)], 3 * 2**20, pinned=True,
    )
    grad_owned = lax.all_to_all(long_grad.reshape(BLOCKS, CHANNELS, LANES), SEQ, 0, 0, tiled=True)

    back_owned = run_kernel(
        backward_kernel, pltpu.HBM(SEQUENCES.shape, BF16),
        [GRID, TURNED, SECTION, TURNED, pltpu.SemaphoreType.DMA], 2,
        grad_owned, pltpu.with_memory_space_constraint(filter_spectrum, pltpu.HBM), steps, unread=(1,),
    )
    filter_grad = run_kernel(
        filter_grad_kernel, jax.ShapeDtypeStruct((CHANNELS, LENGTH), F32), [GRID, TURNED, SECTION], 2,
        grad_owned, product_spectrum, steps, back_owned, unread=(3,),
    )

    quarter = (1, 2, 4, rows, features)
    (share,) = run_blocks(
        mix_kernel, kinds,
        [(mixing.reshape(2, 4, rows, chunk), (2, 1, rows, chunk), 1), (weight, quarter, 0)],
        [((2, 2, 2, rows, features), BF16, (2, 2, 2, rows, features), None)], 6 * 2**20, 2**30,
        [pltpu.VMEM((4, 2 * rows, features), F32)],
    )
    mixed = lax.psum_scatter(
        share.reshape(8 * rows, features), ("xh", "xl", "yl"), scatter_dimension=0, tiled=True
    )

    rim = (2, chunk)
    (query_grad,) = run_blocks(
        query_adjoint, kinds,
        [(query_conv_grad, channels, 0), (shift(query_conv_grad[:, :2].T, -1), rim, 1), (short_taps, taps_block, 2)],
        [((rows, width), BF16, tokens, 1)], 2**20,
    )
    following = shift(jnp.stack([key_conv[:2], value_conv[:2]]), -1)

    back_raw = lax.all_to_all(back_owned, SEQ, 0, 0, tiled=True).reshape(width, rows)
    head, query_grad, filter_grad = lax.optimization_barrier((back_raw[:, :2].T, query_grad, filter_grad))
    after = shift(head, -1)
    grads = run_blocks(
        key_value_adjoint, kinds,
        [(back_raw, channels, 0), (key_conv, tokens, 1), (value_conv, tokens, 1), (short_taps, taps_block, 2)],
        [((rows, width), BF16, tokens, 1)] * 2, 3 * 2**20,
    )
    tail = (RIM, width)
    last = (tail, (rows // RIM - 1, 0))
    key_grad, value_grad = run_blocks(
        key_value_rim, 1,
        [(back_raw[:, rows - RIM :].T, tail, None), (key_conv, last, None), (value_conv, last, None),
         (after, (2, width), None), (following, (2, 2, width), None), (short_taps, (3, 3, width), None),
         (grads[0], None, None), (grads[1], None, None)],
        [((rows, width), BF16, last, None)] * 2, 2**20, alias=((6, 0), (7, 1)),
    )
    return (mixed, query_grad, key_grad, value_grad, filter_grad)


def solution(mesh):
    fine = Mesh(mesh.devices.reshape(tuple(AXES.values())), tuple(AXES))
    token = P(SEQ, TP)
    in_specs = (token, token, token, P(None, None, TP), P(TP + SEQ, None), token, token)
    out_specs = (token, token, token, token, P(TP + SEQ, None))
    return jax.shard_map(
        per_device, mesh=fine, in_specs=in_specs, out_specs=out_specs, check_vma=False
    )
```

```python
import math

import jax
import jax.numpy as jnp
import numpy as np
from jax import lax
from jax.experimental import pallas as pl
from jax.experimental.pallas import tpu as pltpu
from jax.sharding import Mesh
from jax.sharding import PartitionSpec as P

BF16 = jnp.bfloat16
F32 = jnp.float32

AXES = {"xh": 2, "zy": 4, "zh": 2, "zb": 2, "co": 2, "xl": 2, "yh": 2, "yl": 2}
SEQ = ("xh", "zy", "zh", "zb", "co")
TP = ("xl", "yh", "yl")
PLANE = ("xh", "yh", "yl")
COLUMN = ("zy", "zh", "zb", "co")

CHANNELS = 16
BLOCKS = 64
LANES = 128
LENGTH = BLOCKS * LANES
ROWS = BLOCKS * CHANNELS

RIM = 16
VMEM_LIMIT = 20 * 2**20
WHOLE_VMEM = 60 * 2**20


def transform_tables():
    blocks = np.arange(BLOCKS)
    lanes = np.arange(LANES)
    first = 2.0 * np.pi * np.outer(blocks + 0.25, blocks) / BLOCKS
    twist = 2.0 * np.pi * np.outer(blocks + 0.25, lanes) / LENGTH
    second = 2.0 * np.pi * (np.outer(lanes, lanes) % LANES) / LANES
    first_table = np.concatenate([np.cos(first), -np.sin(first)], axis=0)
    cosine, sine = np.cos(second), np.sin(second)
    second_table = np.block([[cosine, -sine], [sine, cosine]])
    steps = np.zeros((2 * LANES + BLOCKS, 5 * LANES))
    steps[: 2 * LANES, : 2 * LANES] = second_table
    steps[: 2 * LANES, 2 * LANES : 4 * LANES] = second_table.T
    steps[: 2 * BLOCKS, 4 * LANES : 4 * LANES + BLOCKS] = first_table
    steps[2 * BLOCKS : 3 * BLOCKS, 4 * LANES : 4 * LANES + 2 * BLOCKS] = first_table.T / LENGTH
    turns = np.concatenate([np.cos(twist), np.sin(twist)], axis=1)
    coarse = turns.astype(BF16).astype(np.float64)
    steps[2 * LANES :, : 2 * LANES] = coarse
    steps[2 * LANES :, 2 * LANES : 4 * LANES] = turns - coarse
    return jnp.asarray(steps, BF16)


def twist_of(steps):
    parts = steps[2 * LANES :].astype(F32)
    turns = parts[:, : 2 * LANES] + parts[:, 2 * LANES : 4 * LANES]
    return turns[:, :LANES], turns[:, LANES:]


def to_spectrum(grid_ref, turned_ref, steps):
    first = steps[: 2 * BLOCKS, 4 * LANES : 4 * LANES + BLOCKS]
    cos_twist, sin_twist = twist_of(steps)
    for c in range(CHANNELS):
        grid = grid_ref[pl.ds(c, BLOCKS, stride=CHANNELS), :].astype(BF16)
        section = jnp.dot(first, grid, preferred_element_type=F32)
        real, imag = section[:BLOCKS], section[BLOCKS:]
        rows = slice(c * BLOCKS, (c + 1) * BLOCKS)
        turned_ref[rows, :LANES] = (real * cos_twist + imag * sin_twist).astype(BF16)
        turned_ref[rows, LANES:] = (imag * cos_twist - real * sin_twist).astype(BF16)
    return jnp.dot(turned_ref[...], steps[: 2 * LANES, : 2 * LANES], preferred_element_type=F32)


def from_spectrum(spectrum, grid_ref, section_ref, steps):
    first_back = steps[2 * BLOCKS : 3 * BLOCKS, 4 * LANES : 4 * LANES + 2 * BLOCKS]
    cos_twist, sin_twist = twist_of(steps)
    section_ref[...] = jnp.dot(
        spectrum, steps[: 2 * LANES, 2 * LANES : 4 * LANES], preferred_element_type=F32
    )
    for c in range(CHANNELS):
        rows = slice(c * BLOCKS, (c + 1) * BLOCKS)
        real, imag = section_ref[rows, :LANES], section_ref[rows, LANES:]
        turned = jnp.concatenate(
            [real * cos_twist - imag * sin_twist, imag * cos_twist + real * sin_twist], axis=0
        ).astype(BF16)
        grid_ref[pl.ds(c, BLOCKS, stride=CHANNELS), :] = jnp.dot(
            first_back, turned, preferred_element_type=F32
        )


def filter_kernel(filter_ref, steps, spectrum_ref, grid, turned):
    for b in range(BLOCKS):
        grid[b * CHANNELS : (b + 1) * CHANNELS, :] = filter_ref[:, b * LANES : (b + 1) * LANES]
    spectrum_ref[...] = to_spectrum(grid, turned, steps).astype(BF16)


def forward_kernel(
    product_ref, filter_spectrum, steps, long_ref, product_spectrum, grid, turned, section
):
    grid[:ROWS] = product_ref[...].astype(F32).reshape(ROWS, LANES)
    own = to_spectrum(grid, turned, steps)
    product_spectrum[...] = own.astype(BF16)
    own_re, own_im = own[:, :LANES], own[:, LANES:]
    other = filter_spectrum[...].astype(F32)
    other_re, other_im = other[:, :LANES], other[:, LANES:]
    turned[:, :LANES] = (own_re * other_re - own_im * other_im).astype(BF16)
    turned[:, LANES:] = (own_re * other_im + own_im * other_re).astype(BF16)
    from_spectrum(turned[...], grid, section, steps)
    long_ref[...] = grid[:ROWS].reshape(BLOCKS, CHANNELS, LANES).astype(BF16)


def correlate(grad_ref, other, grid, turned, section, steps):
    grid[:ROWS] = grad_ref[...].astype(F32).reshape(ROWS, LANES)
    own = to_spectrum(grid, turned, steps)
    own_re, own_im = own[:, :LANES], own[:, LANES:]
    other_re, other_im = other[:, :LANES].astype(F32), other[:, LANES:].astype(F32)
    turned[:, :LANES] = (own_re * other_re + own_im * other_im).astype(BF16)
    turned[:, LANES:] = (own_im * other_re - own_re * other_im).astype(BF16)
    from_spectrum(turned[...], grid, section, steps)


def backward_kernel(grad_ref, filter_spectrum, steps, back_ref, grid, turned, section):
    correlate(grad_ref, filter_spectrum, grid, turned, section, steps)
    back_ref[...] = grid[:ROWS].reshape(BLOCKS, CHANNELS, LANES).astype(BF16)


def filter_grad_kernel(
    grad_ref, product_spectrum, steps, _, filter_grad_ref, grid, turned, section
):
    correlate(grad_ref, product_spectrum, grid, turned, section, steps)
    for b in range(BLOCKS):
        filter_grad_ref[:, b * LANES : (b + 1) * LANES] = grid[
            b * CHANNELS : (b + 1) * CHANNELS, :
        ] * (1.0 / math.sqrt(LENGTH))


SPECTRUM = jax.ShapeDtypeStruct((CHANNELS * BLOCKS, 2 * LANES), BF16)
SEQUENCES = jax.ShapeDtypeStruct((BLOCKS, CHANNELS, LANES), BF16)
GRID = pltpu.VMEM((ROWS + CHANNELS, LANES), F32)
TURNED = pltpu.VMEM((CHANNELS * BLOCKS, 2 * LANES), BF16)
SECTION = pltpu.VMEM((CHANNELS * BLOCKS, 2 * LANES), F32)


def run_kernel(kernel, out_shape, scratch, transforms, *operands, unread=()):
    in_specs = [
        pl.BlockSpec(memory_space=pl.ANY if i in unread else pltpu.VMEM) for i in range(len(operands))
    ]
    transform_flops = 2 * CHANNELS * BLOCKS * LANES * (2 * BLOCKS + 4 * LANES)
    return pl.pallas_call(
        kernel,
        out_shape=out_shape,
        in_specs=in_specs,
        scratch_shapes=scratch,
        compiler_params=pltpu.CompilerParams(vmem_limit_bytes=VMEM_LIMIT),
        cost_estimate=pl.CostEstimate(
            flops=transforms * transform_flops, bytes_accessed=4 * 2**20, transcendentals=0
        ),
    )(*operands)


def run_blocks(kernel, steps, ins, outs, moved, flops=10**6, scratch=(), limit=VMEM_LIMIT, pinned=False, alias=()):
    def spec(block, axis):
        if block is None:
            return pl.BlockSpec(memory_space=axis or pl.ANY)
        fixed = (0,) * len(block)
        if isinstance(block[0], tuple):
            block, fixed = block
        return pl.BlockSpec(block, lambda i: tuple(i if d == axis else fixed[d] for d in range(len(block))))

    return pl.pallas_call(
        kernel,
        grid=(steps,),
        in_specs=[spec(block, axis) for _, block, axis in ins],
        out_specs=[spec(block, axis) for _, _, block, axis in outs],
        out_shape=[
            (pltpu.HBM if pinned else jax.ShapeDtypeStruct)(shape, dtype) for shape, dtype, _, _ in outs
        ],
        input_output_aliases=dict(alias),
        scratch_shapes=list(scratch),
        compiler_params=pltpu.CompilerParams(vmem_limit_bytes=limit),
        cost_estimate=pl.CostEstimate(flops=flops, bytes_accessed=moved, transcendentals=0),
    )(*[array for array, _, _ in ins])


def row_numbers(value):
    return lax.broadcasted_iota(jnp.int32, value.shape, 0)


def causal(value, before, taps):
    number = row_numbers(value)
    one = jnp.where(number == 0, before[1:2], pltpu.roll(value, 1, 0))
    two = jnp.where(number == 0, before[0:1], pltpu.roll(value, 2, 0))
    two = jnp.where(number == 1, before[1:2], two)
    return taps[0:1] * value + taps[1:2] * one + taps[2:3] * two


def adjoint(value, after, taps):
    rows = value.shape[0]
    number = row_numbers(value)
    one = jnp.where(number == rows - 1, after[0:1], pltpu.roll(value, rows - 1, 0))
    two = jnp.where(number == rows - 1, after[1:2], pltpu.roll(value, rows - 2, 0))
    two = jnp.where(number == rows - 2, after[0:1], two)
    return taps[0:1] * value + taps[1:2] * one + taps[2:3] * two


def filter_product(k_ref, v_ref, before_ref, taps_ref, product_ref):
    kc = causal(k_ref[...].astype(F32), before_ref[1].astype(F32), taps_ref[1])
    vc = causal(v_ref[...].astype(F32), before_ref[2].astype(F32), taps_ref[2])
    product_ref[...] = (kc * vc).T.astype(BF16)


def filter_inputs(
    q_ref, k_ref, v_ref, before_ref, taps_ref, _, qc_ref, kc_ref, vc_ref, turned_ref
):
    sources, results = (q_ref, k_ref, v_ref), (qc_ref, kc_ref, vc_ref)
    for i in range(3):
        results[i][...] = causal(sources[i][...].astype(F32), before_ref[i].astype(F32), taps_ref[i])
    turned_ref[...] = qc_ref[...].T


def gate(long_ref, qc_ref, gated_ref):
    gated = (qc_ref[...] * long_ref[...].astype(F32).T).astype(BF16)
    for co in range(2):
        for y in range(4):
            start = (2 * (y % 2) + co) * LANES
            gated_ref[co, y] = gated[:, start : start + LANES]


def partial_kernel(place_ref, gradient_ref, weight_ref, _, out_ref, total):
    xh, xl, yl = place_ref[0], place_ref[1], place_ref[3]
    step = pl.program_id(0)
    features, tokens = gradient_ref.shape[2:]
    rows = tokens // 2
    added = jnp.dot(
        weight_ref[...].reshape(total.shape[0], features),
        gradient_ref[(step // 2) ^ yl, (step % 2) ^ xl],
        preferred_element_type=F32,
    )

    @pl.when(step == 0)
    def _():
        total[...] = added

    @pl.when(step > 0)
    def _():
        total[...] += added

    @pl.when(step == pl.num_programs(0) - 1)
    def _():
        for t in range(2):
            value = total[:, t * rows : (t + 1) * rows].astype(BF16)
            out_ref[t ^ xh] = value.reshape(out_ref.shape[1:])


def long_gradient(parts_ref, qc_ref, long_ref, grad_ref, qg_ref):
    for e in range(2):
        for r in range(2):
            rows = slice((2 * e + r) * LANES, (2 * e + r + 1) * LANES)
            gated_grad = parts_ref[4 * r + e].astype(F32) + parts_ref[4 * r + 2 + e].astype(F32)
            grad_ref[rows] = (qc_ref[rows] * gated_grad).astype(BF16)
            qg_ref[rows] = gated_grad * long_ref[rows].astype(F32)


def mix_kernel(gated_ref, weight_ref, out_ref, total):
    halves, _, rows, width = gated_ref.shape
    features = weight_ref.shape[4]
    step = pl.program_id(0)

    @pl.when(step == 0)
    def _():
        total[...] = jnp.zeros_like(total)

    gated = gated_ref[...].reshape(halves * rows, width)
    for e in range(2):
        for f in range(2):
            total[2 * e + f] += jnp.dot(
                gated, weight_ref[0, :, 2 * e + f].reshape(width, features), preferred_element_type=F32
            )

    @pl.when(step == pl.num_programs(0) - 1)
    def _():
        for e in range(2):
            for f in range(2):
                for t in range(2):
                    out_ref[t, f, e] = total[2 * e + f, t * rows : (t + 1) * rows].astype(BF16)


def query_adjoint(qg_ref, after_ref, taps_ref, out_ref):
    out_ref[...] = adjoint(qg_ref[...].T, after_ref[...], taps_ref[0]).astype(BF16)


def key_value_adjoint(back_ref, kc_ref, vc_ref, taps_ref, key_ref, value_ref):
    back = back_ref[...].astype(F32).T
    after = jnp.zeros((2, back.shape[1]), F32)
    key_ref[...] = adjoint(back * vc_ref[...], after, taps_ref[1]).astype(BF16)
    value_ref[...] = adjoint(back * kc_ref[...], after, taps_ref[2]).astype(BF16)


def key_value_rim(
    tail_ref, kc_ref, vc_ref, after_ref, next_ref, taps_ref, _, __, key_ref, value_ref
):
    back = tail_ref[...].astype(F32)
    after = after_ref[...].astype(F32)
    key_ref[...] = adjoint(back * vc_ref[...], after * next_ref[1], taps_ref[1]).astype(BF16)
    value_ref[...] = adjoint(back * kc_ref[...], after * next_ref[0], taps_ref[2]).astype(BF16)


def shift(value, steps):
    count = 1
    for axis in SEQ:
        count *= lax.axis_size(axis)
    first, last = max(0, -steps), min(count, count - steps)
    return lax.ppermute(value, SEQ, [(i, i + steps) for i in range(first, last)])


def partner(value, axis):
    return lax.ppermute(value, axis, [(0, 1), (1, 0)])


def across(value, dx, dl):
    if not (dx or dl):
        return value
    return lax.ppermute(value, ("xh", "xl"), [(i, i ^ (2 * dx + dl)) for i in range(4)])


def turn(value):
    pairs = []
    for i in range(32):
        a, s, c, b, e = ((i >> k) & 1 for k in (4, 3, 2, 1, 0))
        pairs.append((i, 16 * c + 8 * e + 4 * b + 2 * a + s))
    return lax.ppermute(value, ("xh", "zb", "co", "xl", "yl"), pairs)


def per_device(queries, keys, values, short_taps, long_filter, out_weight, cotangent):
    rows, width = queries.shape
    features = out_weight.shape[1]
    place = jnp.stack([lax.axis_index(axis) for axis in ("xh", "xl", "yh", "yl")])
    place = (place.astype(jnp.int32), None, pltpu.SMEM)
    kinds, chunk = 4, width // 4

    rims = jnp.stack([x[rows - 2 :] for x in (queries, keys, values)])
    rims, out_weight = lax.optimization_barrier((rims, out_weight))
    before, turned = lax.optimization_barrier((shift(rims, 1), turn(out_weight)))
    weight = lax.all_gather(turned, COLUMN, axis=0).reshape(4, 2, 4, rows, features)
    weight = pltpu.with_memory_space_constraint(weight, pltpu.HBM)

    steps = transform_tables()
    filter_spectrum = run_kernel(filter_kernel, SPECTRUM, [GRID, TURNED], 1, long_filter, steps)

    tokens = (rows, chunk)
    channels = (chunk, rows)
    taps_block = (3, 3, chunk)
    plane = ((rows, width), F32, tokens, 1)
    (product,) = run_blocks(
        filter_product, 1,
        [(keys, (rows, width), 1), (values, (rows, width), 1), (before, before.shape, 2), (short_taps, short_taps.shape, 2)],
        [((width, rows), BF16, (width, rows), 0)], 2**20, limit=WHOLE_VMEM,
    )
    query_conv, key_conv, value_conv, query_turned = run_blocks(
        filter_inputs, kinds,
        [(queries, tokens, 1), (keys, tokens, 1), (values, tokens, 1),
         (before, (3, 2, chunk), 2), (short_taps, taps_block, 2), (product, None, None)],
        [plane, plane, plane, ((width, rows), F32, channels, 0)], 3 * 2**20,
    )

    product_owned = lax.all_to_all(product.reshape(BLOCKS, CHANNELS, LANES), SEQ, 0, 0, tiled=True)
    long_owned, product_spectrum = run_kernel(
        forward_kernel, [pltpu.HBM(SEQUENCES.shape, BF16), pltpu.HBM(SPECTRUM.shape, BF16)], [GRID, TURNED, SECTION], 2,
        product_owned, filter_spectrum, steps,
    )
    turned = cotangent.T
    gradient = jnp.stack(
        [jnp.concatenate([across(turned, dx, dl) for dx in range(2)], axis=1) for dl in range(2)]
    )
    gradient = jnp.stack([gradient, partner(gradient, "yl")])

    long_raw = lax.all_to_all(long_owned, SEQ, 0, 0, tiled=True).reshape(width, rows)
    wide, tall = (rows, width // 2), (width // 2, rows)

    (gated,) = run_blocks(
        gate, 2,
        [(long_raw, tall, 0), (query_conv, wide, 1)],
        [((2, 4, rows, chunk), BF16, (2, 4, rows, LANES), 3)], 2 * 2**20, pinned=True,
    )

    mixing = lax.all_to_all(gated.reshape(8, rows, chunk), PLANE, 0, 0, tiled=True)

    (partial,) = run_blocks(
        partial_kernel, kinds,
        [place, (gradient, gradient.shape, None),
         (weight, (4, 2, 1, rows, features), 2), (mixing, None, None)],
        [((2, 4, chunk, rows), BF16, (2, 4, chunk, rows), None)], 6 * 2**20, 2**30,
        [pltpu.VMEM((width, 2 * rows), F32)],
    )
    arrived = lax.all_to_all(partial.reshape(8, chunk, rows), PLANE, 0, 0, tiled=True)
    long_grad, query_conv_grad = run_blocks(
        long_gradient, 2,
        [(arrived, (8, LANES, rows), 1), (query_turned, tall, 0), (long_raw, tall, 0)],
        [((width, rows), BF16, tall, 0), ((width, rows), F32, tall, 0)], 3 * 2**20, pinned=True,
    )
    grad_owned = lax.all_to_all(long_grad.reshape(BLOCKS, CHANNELS, LANES), SEQ, 0, 0, tiled=True)

    back_owned = run_kernel(
        backward_kernel, pltpu.HBM(SEQUENCES.shape, BF16), [GRID, TURNED, SECTION], 2,
        grad_owned, filter_spectrum, steps,
    )
    filter_grad = run_kernel(
        filter_grad_kernel, jax.ShapeDtypeStruct((CHANNELS, LENGTH), F32), [GRID, TURNED, SECTION], 2,
        grad_owned, product_spectrum, steps, back_owned, unread=(3,),
    )

    quarter = (1, 2, 4, rows, features)
    (share,) = run_blocks(
        mix_kernel, kinds,
        [(mixing.reshape(2, 4, rows, chunk), (2, 1, rows, chunk), 1), (weight, quarter, 0)],
        [((2, 2, 2, rows, features), BF16, (2, 2, 2, rows, features), None)], 6 * 2**20, 2**30,
        [pltpu.VMEM((4, 2 * rows, features), F32)],
    )
    mixed = lax.psum_scatter(
        share.reshape(8 * rows, features), ("xh", "xl", "yl"), scatter_dimension=0, tiled=True
    )

    rim = (2, chunk)
    (query_grad,) = run_blocks(
        query_adjoint, kinds,
        [(query_conv_grad, channels, 0), (shift(query_conv_grad[:, :2].T, -1), rim, 1), (short_taps, taps_block, 2)],
        [((rows, width), BF16, tokens, 1)], 2**20,
    )
    following = shift(jnp.stack([key_conv[:2], value_conv[:2]]), -1)

    back_raw = lax.all_to_all(back_owned, SEQ, 0, 0, tiled=True).reshape(width, rows)
    head, query_grad, filter_grad = lax.optimization_barrier((back_raw[:, :2].T, query_grad, filter_grad))
    after = shift(head, -1)
    grads = run_blocks(
        key_value_adjoint, kinds,
        [(back_raw, channels, 0), (key_conv, tokens, 1), (value_conv, tokens, 1), (short_taps, taps_block, 2)],
        [((rows, width), BF16, tokens, 1)] * 2, 3 * 2**20,
    )
    tail = (RIM, width)
    last = (tail, (rows // RIM - 1, 0))
    key_grad, value_grad = run_blocks(
        key_value_rim, 1,
        [(back_raw[:, rows - RIM :].T, tail, None), (key_conv, last, None), (value_conv, last, None),
         (after, (2, width), None), (following, (2, 2, width), None), (short_taps, (3, 3, width), None),
         (grads[0], None, None), (grads[1], None, None)],
        [((rows, width), BF16, last, None)] * 2, 2**20, alias=((6, 0), (7, 1)),
    )
    return (mixed, query_grad, key_grad, value_grad, filter_grad)


def solution(mesh):
    fine = Mesh(mesh.devices.reshape(tuple(AXES.values())), tuple(AXES))
    token = P(SEQ, TP)
    in_specs = (token, token, token, P(None, None, TP), P(TP + SEQ, None), token, token)
    out_specs = (token, token, token, token, P(TP + SEQ, None))
    return jax.shard_map(
        per_device, mesh=fine, in_specs=in_specs, out_specs=out_specs, check_vma=False
    )
```
